32 devices in a mesh: dom: 32 (over z, y, x, core).
Axes of the slice: x: 2, y: 2, z: 4, core: 2. Of those that a mesh axis runs over, the one named last changes fastest.
Arguments:
- dofs: float32 [9, 35, 4096], P(None, None, 'dom'), may hold values from -6 to 6
- star: float32 [3, 9, 9, 4096], P(None, None, None, 'dom'), may hold values from -0.8 to 0.8
- flux_local: float32 [4, 9, 9, 4096], P(None, None, None, 'dom'), may hold values from -0.2 to 0.2
- flux_neigh: float32 [4, 9, 9, 4096], P(None, None, None, 'dom'), may hold values from -0.2 to 0.2
- neighbour: int32 [4, 4096], P(None, 'dom'), may hold values from 0 to 4095, as said below
- neighbour_face: int32 [4, 4096], P(None, 'dom'), may hold values from 0 to 3, as said below
- orientation: int32 [4, 4096], P(None, 'dom'), may hold values from 0 to 2, as said below
- face_kind: int32 [4, 4096], P(None, 'dom'), may hold values from 0 to 2
- cluster: int32 [4096], P('dom'), may hold values from 0 to 2, as said below
- deriv_stiff: float32 [3, 35, 35], replicated, may hold values from -1 to 1
- update_stiff: float32 [3, 35, 35], replicated, may hold values from -0.3125 to 0.3125
- face_proj: float32 [4, 15, 35], replicated, may hold values from -1 to 1
- face_lift: float32 [4, 35, 15], replicated, may hold values from -1.5 to 1.5
- orient_map: float32 [3, 15, 15], replicated, may hold values from -1.5 to 1.5
Outputs:
- advanced: float32 [9, 35, 4096], P(None, None, 'dom')
The draws below stay inside these ranges and needn't reach their ends.
Inputs may be any that keep to these rules, and one draw needn't show every extreme that they name: Each partition (a block of 128 consecutive elements) holds exactly 32 elements of cluster 0, 32 of cluster 1 and 64 of cluster 2. The face relation is symmetric: if face f of element e has neighbour n and neighbour_face g, then face g of n has neighbour e and neighbour_face f, with the same orientation. Across an interior face the neighbour lies in the same partition or in a partition one or two apart along the loop of partitions, wrapping at the ends. Two partitions one apart share at most 64 faces and two partitions two apart at most 32; both bounds are reached. A face of kind 1 or 2 names its own element and its own face. `neighbour_face`: see neighbour. `orientation`: equal on both sides of an interior face; 0 on faces of kinds 1 and 2.
All inputs are finite; a program needn't handle non-finite values.
Results may differ from the reference program's by a relative error of at most 0.0003.
Values sent between devices are 32-bit elements; how exact they have to be, the bound alone decides.
No kernel may reach another device: no remote copies, remote signals or barrier semaphores. Data moves between devices by JAX's collectives and lax.ppermute only.
A program may use at most 128 MiB of HBM per device.

```python
import math
import jax
import jax.numpy as jnp
from jax import lax

ELEM_DEV = 128
FAST_DEV = 32
MIDDLE_DEV = 32
CAP_NEAR = 64
CAP_FAR = 32
ELEMENTS = 4096
QUANTITIES = 9
BASIS = 35
FACE_BASIS = 15
ORDER = 5
SLOTS = 4
N_DOM = 32


def cluster_table(key):
    places = jnp.arange(ELEM_DEV, dtype=jnp.int32)
    pattern = (places >= FAST_DEV).astype(jnp.int32) + (places >= FAST_DEV + MIDDLE_DEV).astype(jnp.int32)
    part_keys = jax.random.split(jax.random.fold_in(key, 201), N_DOM)
    mixing = jax.vmap(lambda single: jax.random.permutation(single, ELEM_DEV))(part_keys).astype(jnp.int32)
    return jnp.take(pattern, mixing).reshape(-1)


def face_graph(key):
    faces = 4 * ELEM_DEV
    parts = jnp.arange(N_DOM, dtype=jnp.int32)[:, None]
    position = jnp.arange(faces, dtype=jnp.int32)[None, :]
    part_keys = jax.random.split(jax.random.fold_in(key, 101), N_DOM)
    layout = jax.vmap(lambda single: jax.random.permutation(single, faces))(part_keys).astype(jnp.int32)
    near = jax.random.randint(jax.random.fold_in(key, 102), (N_DOM,), CAP_NEAR // 2, CAP_NEAR + 1).at[0].set(CAP_NEAR)
    far = jax.random.randint(jax.random.fold_in(key, 103), (N_DOM,), CAP_FAR // 2, CAP_FAR + 1).at[0].set(CAP_FAR)
    edge_one = near
    edge_two = edge_one + jnp.roll(near, 1)
    edge_three = edge_two + far
    edge_four = edge_three + jnp.roll(far, 2)
    border = ELEM_DEV // 4 + jnp.mod(faces - edge_four - ELEM_DEV // 4, 2)
    edge_five = edge_four + border
    first = edge_one[:, None]
    second = edge_two[:, None]
    third = edge_three[:, None]
    fourth = edge_four[:, None]
    fifth = edge_five[:, None]
    seg_one = position < first
    seg_two = (position >= first) & (position < second)
    seg_three = (position >= second) & (position < third)
    seg_four = (position >= third) & (position < fourth)
    seg_five = (position >= fourth) & (position < fifth)
    seg_start = jnp.where(seg_one, 0, jnp.where(seg_two, first, jnp.where(seg_three, second, jnp.where(seg_four, third, jnp.where(seg_five, fourth, fifth)))))
    within = position - seg_start
    partner_part = jnp.where(seg_one, parts + 1, jnp.where(seg_two, parts - 1, jnp.where(seg_three, parts + 2, jnp.where(seg_four, parts - 2, parts + 0 * position))))
    partner_part = jnp.mod(partner_part, N_DOM).astype(jnp.int32)
    paired_local = fifth + jnp.bitwise_xor(within, 1)
    partner_pos = jnp.where(seg_one, jnp.take(edge_one, partner_part) + within, jnp.where(seg_two, within, jnp.where(seg_three, jnp.take(edge_three, partner_part) + within, jnp.where(seg_four, jnp.take(edge_two, partner_part) + within, jnp.where(seg_five, position + 0 * parts, paired_local)))))
    partner_pos = jnp.clip(partner_pos, 0, faces - 1).astype(jnp.int32)
    partner_slot = layout[partner_part, partner_pos]
    turn_one = jax.random.randint(jax.random.fold_in(key, 104), (N_DOM, faces), 0, 3)
    turn_two = jax.random.randint(jax.random.fold_in(key, 105), (N_DOM, faces), 0, 3)
    turn_local = jax.random.randint(jax.random.fold_in(key, 106), (N_DOM, faces), 0, 3)
    clipped = jnp.clip(within, 0, faces - 1)
    rows_all = parts + 0 * position
    back_one = jnp.mod(rows_all - 1, N_DOM)
    back_two = jnp.mod(rows_all - 2, N_DOM)
    turn = jnp.where(seg_one, turn_one[rows_all, clipped], jnp.where(seg_two, turn_one[back_one, clipped], jnp.where(seg_three, turn_two[rows_all, clipped], jnp.where(seg_four, turn_two[back_two, clipped], jnp.where(seg_five, 0, turn_local[rows_all, clipped // 2])))))
    kinds = jnp.where(seg_five, jax.random.randint(jax.random.fold_in(key, 107), (N_DOM, faces), 1, 3), 0)
    neighbour_value = partner_part * ELEM_DEV + partner_slot // 4
    face_value = jnp.mod(partner_slot, 4)
    inverse = jnp.argsort(layout, axis=1, stable=True).astype(jnp.int32)

    def by_slot(values):
        ordered = jnp.take_along_axis(values.astype(jnp.int32), inverse, axis=1)
        return ordered.reshape(N_DOM, ELEM_DEV, 4).transpose(2, 0, 1).reshape(4, N_DOM * ELEM_DEV)
    return (by_slot(neighbour_value), by_slot(face_value), by_slot(turn), by_slot(kinds))


def draw_cluster(key, part):
    return cluster_table(key)


def draw_neighbour(key, part):
    return face_graph(key)[0]


def draw_neighbour_face(key, part):
    return face_graph(key)[1]


def draw_orientation(key, part):
    return face_graph(key)[2]


def draw_face_kind(key, part):
    return face_graph(key)[3]


def draw_star(key, part):
    factor = jnp.exp2(-cluster_table(key).astype(jnp.float32))
    key = jax.random.fold_in(key, 21)
    shape = (3, QUANTITIES, QUANTITIES, ELEMENTS)
    raw = jax.random.truncated_normal(key, -4.0, 4.0, shape, jnp.float32)
    return 0.2 * raw * factor


def draw_flux_local(key, part):
    factor = jnp.exp2(-cluster_table(key).astype(jnp.float32))
    key = jax.random.fold_in(key, 22)
    shape = (4, QUANTITIES, QUANTITIES, ELEMENTS)
    raw = jax.random.truncated_normal(key, -4.0, 4.0, shape, jnp.float32)
    return 0.05 * raw * factor


def draw_flux_neigh(key, part):
    factor = jnp.exp2(-cluster_table(key).astype(jnp.float32))
    key = jax.random.fold_in(key, 23)
    shape = (4, QUANTITIES, QUANTITIES, ELEMENTS)
    raw = jax.random.truncated_normal(key, -4.0, 4.0, shape, jnp.float32)
    return 0.05 * raw * factor


def steps_of(own_key, dims, cuts, smallest, largest):
    level, own = 1.0, jax.random.fold_in(own_key, 6)
    for dim, blocks in cuts:
        heights = jnp.exp(jax.random.uniform(jax.random.fold_in(own, dim), (blocks,), jnp.float32, smallest / len(cuts), largest / len(cuts)))
        level = level * jnp.repeat(heights, dims[dim] // blocks).reshape([-1 if axis == dim else 1 for axis in range(len(dims))])
    return level


def scatter_about(rng, extent, spread, reach, shards=(), kind=jnp.bfloat16):
    array = jax.random.normal(rng, extent, jnp.float32) * spread
    if len(shards) > 0:
        array = steps_of(rng, extent, shards, -0.22, 0.18) * array
    return jnp.clip(array, min=-reach, max=reach).astype(kind)


def setup_inputs(seed: int = 0) -> dict:
    seeds = jax.random.split(jax.random.key(seed), 15)
    dofs = scatter_about(seeds[0], (QUANTITIES, BASIS, ELEMENTS), 1.0, 6.0, ((2, 32),), jnp.float32)
    star = draw_star(jax.random.fold_in(seeds[14], 71), 0)
    flux_local = draw_flux_local(jax.random.fold_in(seeds[14], 71), 0)
    flux_neigh = draw_flux_neigh(jax.random.fold_in(seeds[14], 71), 0)
    neighbour = draw_neighbour(jax.random.fold_in(seeds[14], 71), 0)
    neighbour_face = draw_neighbour_face(jax.random.fold_in(seeds[14], 71), 0)
    orientation = draw_orientation(jax.random.fold_in(seeds[14], 71), 0)
    face_kind = draw_face_kind(jax.random.fold_in(seeds[14], 71), 0)
    cluster = draw_cluster(jax.random.fold_in(seeds[14], 71), 0)
    deriv_stiff = scatter_about(seeds[9], (3, BASIS, BASIS), BASIS ** -0.5, 1.0, (), jnp.float32)
    update_stiff = scatter_about(seeds[10], (3, BASIS, BASIS), (11 * BASIS) ** -0.5, 0.3125, (), jnp.float32)
    face_proj = scatter_about(seeds[11], (4, FACE_BASIS, BASIS), BASIS ** -0.5, 1.0, (), jnp.float32)
    face_lift = scatter_about(seeds[12], (4, BASIS, FACE_BASIS), FACE_BASIS ** -0.5, 1.5, (), jnp.float32)
    orient_map = scatter_about(seeds[13], (3, FACE_BASIS, FACE_BASIS), FACE_BASIS ** -0.5, 1.5, (), jnp.float32)
    return {"dofs": dofs, "star": star, "flux_local": flux_local, "flux_neigh": flux_neigh, "neighbour": neighbour, "neighbour_face": neighbour_face, "orientation": orientation, "face_kind": face_kind, "cluster": cluster, "deriv_stiff": deriv_stiff, "update_stiff": update_stiff, "face_proj": face_proj, "face_lift": face_lift, "orient_map": orient_map}


HIGHEST = lax.Precision.HIGHEST


def taylor_terms(initial, star, deriv_stiff):
    terms = [initial]
    current = initial
    for degree in range(1, ORDER):
        contracted = jnp.einsum("dxy,pye->dpxe", deriv_stiff, current, precision=HIGHEST)
        current = -jnp.einsum("dqpe,dpxe->qxe", star, contracted, precision=HIGHEST)
        terms.append(current)
    return jnp.stack(terms)


def slot_weights(slot_offset):
    weights_list = []
    for degree in range(ORDER):
        upper = jnp.power(slot_offset + 1.0, degree + 1)
        lower = jnp.power(slot_offset, degree + 1)
        weights_list.append((upper - lower) / math.factorial(degree + 1))
    return jnp.stack(weights_list)


def step_weights(step_span):
    return jnp.stack([jnp.power(step_span, degree + 1) / math.factorial(degree + 1) for degree in range(ORDER)])


def weighted_sum(terms, weights):
    return jnp.sum(terms * weights[:, None, None, :], axis=0)


def update_state(fields, taylor, collected, star, flux_local, flux_neigh, orientation, face_kind, step_span, update_stiff, face_proj, face_lift, orient_map):
    step_integral = weighted_sum(taylor, step_weights(step_span))
    contracted = jnp.einsum("pye,dyx->dpxe", step_integral, update_stiff, precision=HIGHEST)
    volume = jnp.einsum("dqpe,dpxe->qxe", star, contracted, precision=HIGHEST)
    own_faces = jnp.einsum("fmb,qbe->qmfe", face_proj, step_integral, precision=HIGHEST)
    rotated = jnp.zeros_like(collected)
    for rotation in range(3):
        selected = (orientation == rotation).astype(jnp.float32)
        rotated = rotated + selected * jnp.einsum("mn,qnfe->qmfe", orient_map[rotation], collected, precision=HIGHEST)
    mirror_signs = jnp.where(jnp.arange(QUANTITIES) < 6, -1.0, 1.0).astype(jnp.float32)
    mirrored = mirror_signs[:, None, None, None] * own_faces
    outside = jnp.where(face_kind == 0, rotated, jnp.where(face_kind == 1, mirrored, jnp.zeros_like(mirrored)))
    face_terms = jnp.einsum("fqpe,pmfe->qmfe", flux_local, own_faces, precision=HIGHEST)
    face_terms = face_terms + jnp.einsum("fqpe,pmfe->qmfe", flux_neigh, outside, precision=HIGHEST)
    lifted = jnp.einsum("fbm,qmfe->qbe", face_lift, face_terms, precision=HIGHEST)
    return fields + volume - lifted


def reference(dofs, star, flux_local, flux_neigh, neighbour, neighbour_face, orientation, face_kind, cluster, deriv_stiff, update_stiff, face_proj, face_lift, orient_map):
    element_total = dofs.shape[2]
    by_cluster = jnp.argsort(cluster, stable=True).astype(jnp.int32)
    levels = (FAST_DEV * N_DOM, (FAST_DEV + MIDDLE_DEV) * N_DOM, ELEM_DEV * N_DOM)
    span_whole = jnp.left_shift(jnp.ones_like(cluster), cluster).astype(jnp.int32)
    step_span = span_whole.astype(jnp.float32)
    source = (neighbour_face * element_total + neighbour).reshape(-1).astype(jnp.int32)
    fields = dofs
    taylor = jnp.zeros((ORDER,) + dofs.shape, jnp.float32)
    collected = jnp.zeros((QUANTITIES, FACE_BASIS, 4, element_total), jnp.float32)
    for slot_index in range(SLOTS):
        first_level = max(level for level in range(3) if slot_index % (2 ** level) == 0)
        last_level = max(level for level in range(3) if (slot_index + 1) % (2 ** level) == 0)
        starters = by_cluster[:levels[first_level]]
        renewed_terms = taylor_terms(jnp.take(fields, starters, axis=2), jnp.take(star, starters, axis=3), deriv_stiff)
        taylor = taylor.at[:, :, :, starters].set(renewed_terms)
        slot_offset = jnp.mod(slot_index, span_whole).astype(jnp.float32)
        integral = weighted_sum(taylor, slot_weights(slot_offset))
        face_values = jnp.einsum("gmb,qbe->qmge", face_proj, integral, precision=HIGHEST)
        face_values = face_values.reshape(QUANTITIES * FACE_BASIS, 4 * element_total)
        collected = collected + jnp.take(face_values, source, axis=1).reshape(QUANTITIES, FACE_BASIS, 4, element_total)
        finished = by_cluster[:levels[last_level]]
        renewed = update_state(
            jnp.take(fields, finished, axis=2), jnp.take(taylor, finished, axis=3), jnp.take(collected, finished, axis=3),
            jnp.take(star, finished, axis=3), jnp.take(flux_local, finished, axis=3), jnp.take(flux_neigh, finished, axis=3),
            jnp.take(orientation, finished, axis=1), jnp.take(face_kind, finished, axis=1), jnp.take(step_span, finished, axis=0),
            update_stiff, face_proj, face_lift, orient_map)
        fields = fields.at[:, :, finished].set(renewed)
        collected = collected.at[:, :, :, finished].set(0.0)
    return fields
```

```python
import functools
import math
import types

import jax
import jax.numpy as jnp
from jax import lax
from jax.experimental import pallas as pl
from jax.experimental.pallas import tpu as pltpu
from jax.sharding import PartitionSpec as P

CAP_NEAR = 64
CAP_FAR = 32
QUANTITIES = 9
BASIS = 35
BASIS_PAD = 40
FACE_BASIS = 15
FACE_PAD = 16
FACES = 4
ORDER = 5
SLOTS = 4
LANES = 128
FACE_ROWS = QUANTITIES * FACE_PAD
SEND_ROWS = 80
PACK = 32
GROUPS = LANES // PACK
PACKS = 3

OFFSETS = (1, -1, 2, -2)
SEND_ORDER = (2, 1, 3, 0)
F32 = jnp.float32
BF16 = jnp.bfloat16
VMEM = pl.BlockSpec(memory_space=pltpu.VMEM)
NAMES = ("sent_a", "sent_x", "sent_y", "sent_z")


def exchange(sends):
    devices = lax.axis_size("dom")
    receives = {}
    for partner in SEND_ORDER:
        by = OFFSETS[partner]
        pairs = [(i, (i + (by if i % 2 == 0 else -by)) % devices) for i in range(devices)]
        receives[RECEIVED[partner]] = lax.ppermute(sends[NAMES[partner]], "dom", pairs)
    return receives


def split(x):
    high = x.astype(BF16).astype(F32)
    return high, x - high


def wide_basis(matrix):
    high, low = split(matrix)
    return high + pltpu.roll(high, 40, 1) + pltpu.roll(low, 80, 1)


def tall_basis(x):
    high, low = split(x)
    rest = jnp.zeros((LANES - 3 * BASIS_PAD, x.shape[1]), F32)
    return jnp.concatenate([high, low, high, rest], axis=0).astype(BF16)


def wide_faces(matrix):
    high, low = split(matrix)
    return jnp.concatenate([high + pltpu.roll(high, 64, 1), low], axis=1)


def tall_faces(x):
    high, low = split(x)
    return jnp.concatenate([high, low, high], axis=0).astype(BF16)


def matmul(left, right):
    return jnp.dot(left.astype(BF16), right, preferred_element_type=F32)


def side_by_side(pieces):
    return jnp.concatenate(pieces, axis=1)


def lanes_of(q):
    return slice(q * LANES, (q + 1) * LANES)


def star_tile(star, work, quantities, groups):
    total = [None] * len(quantities)
    for d in range(3):
        for p in range(groups):
            piece = work[d * BASIS_PAD : (d + 1) * BASIS_PAD, lanes_of(p)]
            for i, q in enumerate(quantities):
                term = star[q, p, d : d + 1, :] * piece
                total[i] = term if total[i] is None else total[i] + term
    return total


def apply_star(star, work, put):
    for first in range(0, QUANTITIES, 3):
        for i, value in enumerate(star_tile(star, work, range(first, first + 3), QUANTITIES)):
            put(first + i, value)


def apply_flux(flux, faces, lift_in):
    for f in range(FACES):
        total = [None] * QUANTITIES
        for p in range(QUANTITIES):
            piece = faces(f, p)
            for q in range(QUANTITIES):
                term = flux[q, p, f : f + 1, :] * piece
                total[q] = term if total[q] is None else total[q] + term
        for q in range(QUANTITIES):
            lift_in[f * FACE_PAD : (f + 1) * FACE_PAD, lanes_of(q)] = total[q]


def lift(lift_w, lift_in):
    right = side_by_side([tall_faces(lift_in[:, lanes_of(q)]) for q in range(QUANTITIES)])
    return matmul(lift_w[0:48, :192], right)


def predict(taylor, star, deriv_w, works):
    for k in range(ORDER):
        for first in range(0, QUANTITIES, 3):
            if k:
                values = star_tile(star, works[k % 2], range(first, first + 3), QUANTITIES)
                for i in range(3):
                    taylor[k, first + i] = values[i]
            else:
                values = [taylor[0, first + i] for i in range(3)]
            if k < ORDER - 1:
                right = side_by_side([tall_basis(value) for value in values])
                works[(k + 1) % 2][:, first * LANES : (first + 3) * LANES] = matmul(deriv_w[...], right)


def integral(taylor, q, j):
    total = None
    for k in range(ORDER):
        weight = ((j + 1) ** (k + 1) - j ** (k + 1)) / math.factorial(k + 1)
        term = taylor[k, q] * weight
        total = term if total is None else total + term
    return total


def step_integral(taylor, q, span):
    total = None
    power = span
    for k in range(ORDER):
        term = taylor[k, q] * (power * (1.0 / math.factorial(k + 1)))
        total = term if total is None else total + term
        power = power * span
    return total


def rotated_faces(turn_w, orientation, integrals, put):
    right = side_by_side([tall_basis(value) for value in integrals])
    result = matmul(turn_w[...], right)
    for g in range(FACES):
        turn = orientation[g : g + 1, :]
        for q in range(QUANTITIES):
            parts = []
            for o in range(3):
                first = (o * FACES + g) * FACE_PAD
                parts.append(result[first : first + FACE_PAD, lanes_of(q)])
            put(g, q, jnp.where(turn == 0, parts[0], jnp.where(turn == 1, parts[1], parts[2])))


def rows_of(q):
    return slice(q * FACE_PAD, (q + 1) * FACE_PAD)


def take_lanes(source, index):
    if source.shape[0] == 1:
        return take_lanes(jnp.broadcast_to(source, (8, LANES)), index)[0:1, :]
    return jnp.take_along_axis(source, jnp.broadcast_to(index, source.shape), axis=1)


def turn_lanes(x, shift):
    return pltpu.roll(x, shift % LANES, 1) if shift % LANES else x


def choose(pieces, lane, width):
    total = pieces[0]
    for j in range(1, len(pieces)):
        total = jnp.where(lane // width == j, pieces[j], total)
    return total


def pack_sends(faces, index, sends):
    tiles = []
    for row in (0, 2):
        lane = index[row : row + 1, :]
        face = index[row + 1 : row + 2, :]
        tile = take_lanes(faces[0], lane)
        for g in range(1, FACES):
            tile = jnp.where(face == g, take_lanes(faces[g], lane), tile)
        tiles.append(tile)
    lane = lax.broadcasted_iota(jnp.int32, (FACE_PAD, LANES), 1)
    nothing = jnp.zeros((FACE_PAD, LANES), F32)

    def piece(tile, q):
        return tiles[tile][rows_of(q), :] if q < QUANTITIES else nothing

    for k in range(5):
        low, high = piece(0, 2 * k), piece(0, 2 * k + 1)
        sends[0][rows_of(k), :] = choose([low, turn_lanes(high, 64)], lane, 64)
        sends[1][rows_of(k), :] = choose([turn_lanes(low, 64), high], lane, 64)
    for k in range(5):
        for side in range(2):
            value = nothing
            if k < PACKS:
                parts = [turn_lanes(piece(1, 4 * k + j), 32 * j - 64 * side) for j in range(4)]
                value = choose(parts, lane, 32)
            sends[2 + side][rows_of(k), :] = value


def unpack_receives(receives, near, far):
    lane = lax.broadcasted_iota(jnp.int32, (FACE_PAD, LANES), 1)
    for q in range(QUANTITIES):
        ahead, behind = receives[0][rows_of(q // 2), :], receives[1][rows_of(q // 2), :]
        shift = 64 * (q % 2)
        near[rows_of(q), :] = choose([turn_lanes(ahead, shift), turn_lanes(behind, 64 + shift)], lane, 64)
        ahead, behind = receives[2][rows_of(q // 4), :], receives[3][rows_of(q // 4), :]
        shift = -32 * (q % 4)
        far[rows_of(q), :] = choose([turn_lanes(ahead, shift), turn_lanes(behind, 64 + shift)], lane, 64)


def add_remote(index, near, far, collected, put):
    for f in range(FACES):
        place = index[f : f + 1, :]
        lane = jnp.bitwise_and(place, LANES - 1)
        from_near = take_lanes(near[...], lane)
        from_far = take_lanes(far[...], lane)
        remote = jnp.where(place >= LANES, from_far, jnp.where(place >= 0, from_near, 0.0))
        put(f, collected[f] + remote)


def transposed(rows, flip):
    flip[...] = jnp.zeros((LANES, LANES), F32)
    for f in range(FACES):
        flip[f : f + 1, :] = rows[f]
    return flip[...].T


def ranks(keys, flip):
    columns = transposed(keys, flip)
    result = []
    for f in range(FACES):
        total = None
        for other in range(FACES):
            less = jnp.where(columns[:, other : other + 1] < keys[f], 1.0, 0.0)
            total = less if total is None else total + less
        result.append(jnp.sum(total, axis=0, keepdims=True))
    return result


def group_places(groups, keys, flip):
    bases = (0.0, 64.0, 128.0, 192.0)
    order = ranks([groups[f] * 512.0 + keys[f] for f in range(FACES)], flip)
    sizes = []
    for partner in range(FACES):
        total = None
        for f in range(FACES):
            here = jnp.where(groups[f] == partner, 1.0, 0.0)
            total = here if total is None else total + here
        sizes.append(jnp.sum(total, axis=1, keepdims=True))
    places = []
    for f in range(FACES):
        place = jnp.full((1, LANES), -1.0, F32)
        start = jnp.zeros((1, 1), F32)
        for partner in range(FACES):
            place = jnp.where(groups[f] == partner, order[f] - start + bases[partner], place)
            start = start + sizes[partner]
        places.append(place)
    return places


def partner_groups(devices, neighbour, face_kind):
    here = lax.axis_index("dom")
    sign = 1 - 2 * jnp.bitwise_and(here, 1)
    targets = [jnp.where(sign * by < 0, sign * by + devices, sign * by) for by in OFFSETS]
    sources = targets[:2] + [devices - far for far in targets[2:]]
    send_groups, recv_groups, local = [], [], []
    for f in range(FACES):
        interior = face_kind[f : f + 1, :] == 0
        distance = lax.shift_right_logical(neighbour[f : f + 1, :], 7) - here
        distance = jnp.where(distance < 0, distance + devices, distance)
        send = jnp.full((1, LANES), 4, jnp.int32)
        recv = jnp.full((1, LANES), 4, jnp.int32)
        for partner in range(4):
            send = jnp.where(interior & (distance == targets[partner]), partner, send)
            recv = jnp.where(interior & (distance == sources[partner]), partner, recv)
        send_groups.append(send.astype(F32))
        recv_groups.append(recv.astype(F32))
        local.append(interior & (distance == 0))
    return send_groups, recv_groups, local


def make_send_index(devices, neighbour, face_kind, index, flip):
    groups, _, _ = partner_groups(devices, neighbour, face_kind)
    element = lax.broadcasted_iota(jnp.int32, (1, LANES), 1)
    keys = [(element + f * LANES).astype(F32) for f in range(FACES)]
    places = group_places(groups, keys, flip)
    for tile, (element, face) in enumerate(columns_of(places, flip)):
        index[2 * tile : 2 * tile + 1, :] = element
        index[2 * tile + 1 : 2 * tile + 2, :] = face


def columns_of(places, flip):
    columns = transposed(places, flip)
    row = lax.broadcasted_iota(jnp.int32, (LANES, LANES), 0).astype(F32)
    lane = lax.broadcasted_iota(jnp.int32, (LANES, LANES), 1).astype(F32)
    result = []
    for tile in range(2):
        total = None
        for f in range(FACES):
            hit = jnp.where(columns[:, f : f + 1] == lane + tile * 128.0, row + f * 128.0, 0.0)
            total = hit if total is None else total + hit
        code = jnp.sum(total, axis=0, keepdims=True).astype(jnp.int32)
        result.append((jnp.bitwise_and(code, LANES - 1), lax.shift_right_logical(code, 7)))
    return result


def make_recv_index(devices, neighbour, neighbour_face, face_kind, index, flip):
    _, groups, local = partner_groups(devices, neighbour, face_kind)
    index[...] = jnp.zeros((24, LANES), jnp.int32)
    keys = []
    for f in range(FACES):
        far_face = neighbour_face[f : f + 1, :]
        far_element = jnp.bitwise_and(neighbour[f : f + 1, :], LANES - 1)
        keys.append((far_face * LANES + far_element).astype(F32))
        index[8 + f : 9 + f, :] = far_element
        index[16 + f : 17 + f, :] = jnp.where(local[f], far_face, -1)
    places = group_places(groups, keys, flip)
    for f in range(FACES):
        index[f : f + 1, :] = places[f].astype(jnp.int32)


def make_deriv(deriv, frame, deriv_w):
    deriv_w[...] = frame[...]
    for d in range(3):
        deriv_w[d * BASIS_PAD : d * BASIS_PAD + BASIS, :BASIS] = -deriv[d]
    deriv_w[...] = wide_basis(deriv_w[...])


def make_faces(proj, orient, frame, proj_w, turn_w, flip):
    proj_w[...] = frame[0:64, :]
    for g in range(FACES):
        proj_w[g * FACE_PAD : g * FACE_PAD + FACE_BASIS, :BASIS] = proj[:, g, :]
    right = side_by_side([proj_w[rows_of(g), :] for g in range(FACES)])
    flip[...] = frame[...]
    for o in range(3):
        flip[o * FACE_PAD : o * FACE_PAD + FACE_BASIS, :FACE_BASIS] = orient[o]
    turned = jnp.dot(
        flip[0:48, :FACE_PAD], right, precision=lax.Precision.HIGHEST, preferred_element_type=F32
    )
    for o in range(3):
        for g in range(FACES):
            turn_w[rows_of(o * FACES + g), :] = wide_basis(turned[rows_of(o), lanes_of(g)])
    proj_w[...] = wide_basis(proj_w[...])


def make_update(update, update_w, flip):
    update_w[...] = jnp.zeros((LANES, LANES), F32)
    for d in range(3):
        flip[...] = jnp.zeros((LANES, LANES), F32)
        flip[:BASIS, :BASIS] = update[d]
        update_w[d * BASIS_PAD : (d + 1) * BASIS_PAD, :] = flip[...].T[:BASIS_PAD, :]
    update_w[...] = wide_basis(update_w[...])


def make_lift(lift_mat, deriv_w, lift_w, flip):
    total = None
    for f in range(FACES):
        flip[...] = jnp.zeros((LANES, LANES), F32)
        flip[:FACE_BASIS, :BASIS] = lift_mat[:, f, :]
        value = turn_lanes(flip[...].T[0:48, :], 16 * f)
        total = value if total is None else total + value
    lift_w[0:48, :] = wide_faces(total)
    lift_w[48:176, :] = wide_faces(matmul(deriv_w[...], tall_basis(total[0:BASIS_PAD, :])))


def pack(pieces, element, lane):
    return choose([take_lanes(piece, element) for piece in pieces], lane, PACK)


def pack_quantities(pieces, element):
    lane = lax.broadcasted_iota(jnp.int32, pieces[0].shape, 1)
    nothing = jnp.zeros(pieces[0].shape, F32)
    result = []
    for k in range(PACKS):
        group = [take_lanes(pieces[q], element) if q < QUANTITIES else nothing for q in range(4 * k, 4 * k + 4)]
        result.append(choose(group, lane, PACK))
    return result


def unpack_quantity(packed, q, rank):
    return take_lanes(packed(q // 4), rank + PACK * (q % 4))


def make_packs(r):
    row = lax.broadcasted_iota(jnp.int32, (LANES, LANES), 0).astype(F32)
    lane = lax.broadcasted_iota(jnp.int32, (LANES, LANES), 1)
    cluster = r.cluster[...].astype(F32)
    columns = transposed([cluster] * FACES, r.flip)
    before = jnp.where((columns[:, 0:1] == cluster) & (row < lane.astype(F32)), 1.0, 0.0)
    rank = jnp.sum(before, axis=0, keepdims=True)
    columns = transposed([cluster * 64.0 + rank] * FACES, r.flip)
    r.packs[...] = jnp.zeros((8, LANES), jnp.int32)
    for block in range(2):
        wanted = jnp.bitwise_and(lane, PACK - 1).astype(F32) + 64.0 * block
        hit = jnp.where(columns[:, 0:1] == wanted, row, 0.0)
        r.packs[block : block + 1, :] = jnp.sum(hit, axis=0, keepdims=True).astype(jnp.int32)
    rank = rank.astype(jnp.int32)
    r.packs[2:3, :] = jnp.bitwise_and(rank, PACK - 1)
    lane = lax.broadcasted_iota(jnp.int32, (1, LANES), 1)
    kinds = r.cluster[...]
    for f in range(FACES):
        r.source_cluster[f : f + 1, :] = take_lanes(kinds, r.index[8 + f : 9 + f, :])
    got = [r.index[f : f + 1, :].astype(F32) for f in range(FACES)]
    for tile, (element, _) in enumerate(columns_of(got, r.flip)):
        kind = take_lanes(kinds, element)
        for side in range(2):
            width = 32 if tile else 64
            parts = [turn_lanes(kind, width * j - 64 * side) for j in range(LANES // width)]
            first = 2 * tile + side
            r.column_cluster[first : first + 1, :] = choose(parts, lane, width)
    for tile in range(2):
        element = r.send_index[2 * tile : 2 * tile + 1, :]
        face = r.send_index[2 * tile + 1 : 2 * tile + 2, :]
        kind = take_lanes(kinds, element)
        order = take_lanes(jnp.bitwise_and(rank, PACK - 1), element)
        rows = [order] + [jnp.where(kind == block, face, -1) for block in range(2)]
        for side in range(2):
            width = 32 if tile else 64
            for i in range(3):
                parts = [turn_lanes(rows[i], width * j - 64 * side) for j in range(LANES // width)]
                value = choose(parts, lane, width)
                if i == 0:
                    value = value + PACK * (lane // width)
                first = 3 * (2 * tile + side) + i
                r.send_packs[first : first + 1, :] = value


def pack_flux(flux, element, packed):
    lane = lax.broadcasted_iota(jnp.int32, (FACES, LANES), 1)
    face = lax.broadcasted_iota(jnp.int32, (FACES, LANES), 0)
    for q in range(QUANTITIES):
        for p in range(QUANTITIES):
            value = jnp.where(face == lane // PACK, take_lanes(flux[q, p], element), 0.0)
            packed[q, p : p + 1, :] = jnp.sum(value, axis=0, keepdims=True)


def pack_block(r, block, where, star, flux):
    element = r.packs[block : block + 1, :]
    lane = lax.broadcasted_iota(jnp.int32, (1, LANES), 1)
    where[...] = jnp.zeros((8, LANES), jnp.int32)
    where[0:1, :] = pack([r.index[f : f + 1, :] for f in range(FACES)], element, lane)
    where[1:5, :] = take_lanes(r.orientation[...], element)
    where[5:6, :] = pack([r.index[8 + f : 9 + f, :] for f in range(FACES)], element, lane)
    where[6:7, :] = pack([r.index[16 + f : 17 + f, :] for f in range(FACES)], element, lane)
    for q in range(QUANTITIES):
        for k, value in enumerate(pack_quantities([r.star[q, p] for p in range(QUANTITIES)], element)):
            star[q, k] = value
    pack_flux(r.flux_neigh, element, flux)


def spread_faces(total, lift_in):
    lane = lax.broadcasted_iota(jnp.int32, (FACE_PAD, LANES), 1)
    nothing = jnp.zeros((FACE_PAD, LANES), F32)
    for k in range(PACKS):
        for f in range(FACES):
            parts = []
            for j in range(GROUPS):
                q = GROUPS * k + j
                parts.append(turn_lanes(total[q], PACK * (j - f)) if q < QUANTITIES else nothing)
            lift_in[f * FACE_PAD : (f + 1) * FACE_PAD, lanes_of(k)] = choose(parts, lane, PACK)
    return side_by_side([tall_faces(lift_in[:, lanes_of(k)]) for k in range(PACKS)])


def packed_fields(r, base, ahead, gathered, flux, where, lift_in, work):
    place = where[0:1, :]
    near = jnp.bitwise_and(place, 63)
    far = jnp.bitwise_and(place, PACK - 1)
    total = [None] * QUANTITIES
    for p in range(QUANTITIES):
        got = [take_lanes(ref[rows_of(p // 2), :], near + 64 * (p % 2)) for ref in (r.sum_a, r.sum_x)]
        got += [take_lanes(ref[rows_of(p // 4), :], far + PACK * (p % 4)) for ref in (r.sum_y, r.sum_z)]
        remote = jnp.where(place < 64, got[0], jnp.where(place < 128, got[1], jnp.where(place < 192, got[2], got[3])))
        piece = gathered[rows_of(p), :] + jnp.where(place >= 0, remote, 0.0)
        for q in range(QUANTITIES):
            term = flux[q, p : p + 1, :] * piece
            total[q] = term if total[q] is None else total[q] + term
    right = spread_faces(total, lift_in)
    lifted = matmul(r.lift_w[:, :192], right)
    work[...] = ahead[...] - lifted[48:176, :]
    return [base[k] - lifted[:BASIS_PAD, lanes_of(k)] for k in range(PACKS)]


def packed_derivatives(terms, deriv_w, work):
    for k in range(PACKS):
        work[:, lanes_of(k)] = matmul(deriv_w[...], tall_basis(terms[k]))


def gather_copies(values):
    lane = lax.broadcasted_iota(jnp.int32, (BASIS_PAD, LANES), 1)
    if len(values) == 1:
        total = values[0] + pltpu.roll(values[0], 64, 1)
        return jnp.where(lane < PACK, total + pltpu.roll(total, 96, 1), 0.0)
    low = lane < 64
    halves = []
    for i in range(2):
        a, b = values[i], values[i + 2]
        halves.append(jnp.where(low, a, b) + pltpu.roll(jnp.where(low, b, a), 64, 1))
    even = jnp.bitwise_and(lane, PACK) == 0
    swapped = take_lanes(jnp.where(even, halves[1], halves[0]), jnp.bitwise_xor(lane[0:1, :], PACK))
    return jnp.where(even, halves[0], halves[1]) + swapped


def packed_star(star, work, follow=None):
    result = []
    for k in range(PACKS):
        quantities = range(GROUPS * k, min(GROUPS * (k + 1), QUANTITIES))
        result.append(gather_copies(star_tile(star, work, quantities, PACKS)))
        if follow is not None:
            follow(k, result[k])
    return result


def packed_faces(integrals, turn_w, where, put):
    right = side_by_side([tall_basis(value) for value in integrals])
    result = matmul(turn_w[...], right)
    for g in range(FACES):
        turn = where[1 + g : 2 + g, :]
        for k in range(PACKS):
            parts = [result[rows_of(o * FACES + g), lanes_of(k)] for o in range(3)]
            put(g, k, jnp.where(turn == 0, parts[0], jnp.where(turn == 1, parts[1], parts[2])))


def add_terms(total, terms, weight):
    values = [term * weight for term in terms]
    return values if total is None else [a + b for a, b in zip(total, values)]


def add_received(r):
    for name in "axyz":
        getattr(r, "sum_" + name)[...] = getattr(r, "got_" + name)[...] + getattr(r, "old_" + name)[...]


def slot_kernel(slot, r):
    add_received(r)
    numbers = (0, 1) if slot == 2 else (0,)
    names = ("base", "ahead", "gathered", "flux", "where", "lift_in", "star", "fields", "step", "faces", "work", "spare")
    blocks = [types.SimpleNamespace(**{name: getattr(r, name + str(b)) for name in names}) for b in numbers]
    terms = []
    for block in blocks:
        terms.append(
            packed_fields(
                r, block.base, block.ahead, block.gathered, block.flux, block.where, block.lift_in, block.work
            )
        )
        for k in range(PACKS):
            block.fields[k] = terms[-1][k]
    first = [None] * len(blocks)
    second = None
    for k in range(ORDER):
        for b, block in enumerate(blocks):
            if k:
                work, other = (block.work, block.spare) if k % 2 else (block.spare, block.work)

                def follow(i, value, other=other):
                    other[:, lanes_of(i)] = matmul(r.deriv_w[...], tall_basis(value))

                terms[b] = packed_star(block.star, work, follow if k < ORDER - 1 else None)
            first[b] = add_terms(first[b], terms[b], 1.0 / math.factorial(k + 1))
        if slot == 2:
            second = add_terms(second, terms[1], (2.0 ** (k + 1) - 1.0) / math.factorial(k + 1))
    for b, block in enumerate(blocks):

        def put(g, k, value, faces=block.faces):
            faces[g, rows_of(k), :] = value

        packed_faces(first[b], r.turn_w, block.where, put)
        for k in range(PACKS):
            block.step[k] = first[b][k]
    if slot == 2:
        for k in range(PACKS):
            r.second1[k] = second[k]
    for partner in SEND_ORDER:
        later, sent = getattr(r, "later_" + NAMES[partner]), getattr(r, NAMES[partner])
        near = partner < 2
        lane = r.send_packs[3 * partner : 3 * partner + 1, :]
        for k in range(5 if near else PACKS):
            value = later[rows_of(k), :]
            source = k // 2 if near else k
            place = lane + 64 * (k % 2) if near else lane
            for b, block in enumerate(blocks):
                face = r.send_packs[3 * partner + 1 + b : 3 * partner + 2 + b, :]
                for g in range(FACES):
                    value = jnp.where(face == g, take_lanes(block.faces[g, rows_of(source), :], place), value)
            sent[rows_of(k), :] = value
        if not near:
            sent[48:80, :] = jnp.zeros((32, LANES), F32)


def frame_kernel(r):
    r.frame[...] = jnp.zeros((LANES, LANES), F32)


def prepare_kernel(devices, r):
    r.orientation_out[...] = r.orientation[...]
    r.cluster_out[...] = r.cluster[...].reshape(1, LANES)
    r.far_out[...] = r.neighbour_face[...]
    make_send_index(devices, r.neighbour, r.face_kind, r.send_index, r.flip)
    make_deriv(r.deriv, r.frame, r.deriv_w)
    make_faces(r.proj, r.orient, r.frame, r.proj_w, r.turn_w, r.flip)


def first_kernel(r):
    for q in range(QUANTITIES):
        r.taylor[0, q] = jnp.zeros((BASIS_PAD, LANES), F32)
        r.taylor[0, q, :BASIS, :] = r.dofs[q]
    predict(r.taylor, r.star, r.deriv_w, (r.spare, r.work))
    span = lax.shift_left(jnp.ones_like(r.cluster[...]), r.cluster[...]).astype(F32)
    for q in range(QUANTITIES):
        r.step[q] = step_integral(r.taylor, q, span)

    def put(g, q, value):
        r.faces[g, rows_of(q), :] = value

    rotated_faces(r.turn_w, r.orientation, [integral(r.taylor, q, 0) for q in range(QUANTITIES)], put)
    pack_sends(r.faces, r.send_index, [getattr(r, name) for name in NAMES])


def last_kernel(r):
    add_received(r)
    unpack_receives([r.sum_a, r.sum_x, r.sum_y, r.sum_z], r.near, r.far)

    def keep(f, value):
        r.collected[f] = value

    add_remote(r.index, r.near, r.far, r.gathered, keep)
    apply_flux(r.flux_neigh, lambda f, p: r.collected[f, rows_of(p), :], r.lift_in)
    lifted = lift(r.lift_w, r.lift_in)
    for q in range(QUANTITIES):
        r.out[q] = (r.base[q] - lifted[:BASIS_PAD, lanes_of(q)])[:BASIS, :]


def beside_kernel(slot, devices, r):
    if slot == 0:
        make_update(r.update, r.update_w, r.flip)
        make_lift(r.lift_mat, r.deriv_w, r.lift_w, r.flip)
        make_recv_index(devices, r.neighbour, r.neighbour_face, r.face_kind, r.index, r.flip)
        make_packs(r)
        pack_block(r, 0, r.where0, r.star0, r.flux0)
        mirror = jnp.where(r.face_kind[...] == 1, 1.0, 0.0)
        for p in range(QUANTITIES):
            sign = -mirror if p < 6 else mirror
            for q in range(QUANTITIES):
                r.flux_own[q, p] = r.flux_local[q, p] + sign * r.flux_neigh[q, p]
    cluster = r.cluster[...]
    started = cluster <= (0 if slot % 2 else 1)
    rank = r.packs[2:3, :]

    def unpacked(name, q, rows=None):
        def packed(ref):
            return (lambda k: ref[k]) if rows is None else (lambda k: ref[rows, rows_of(k), :])

        value = unpack_quantity(packed(getattr(r, name + "0")), q, rank)
        if slot == 2:
            value = jnp.where(cluster == 1, unpack_quantity(packed(getattr(r, name + "1")), q, rank), value)
        return value

    sums = r.sums
    for g in range(FACES):
        reset = r.source_cluster[g : g + 1, :] <= (0 if slot % 2 else 1)
        for q in range(QUANTITIES):
            if slot == 0:
                sums[g, rows_of(q), :] = r.faces[g, rows_of(q), :]
                continue
            value = jnp.where(started, unpacked("faces", q, g), r.later[g, rows_of(q), :])
            sums[g, rows_of(q), :] = value + jnp.where(reset, 0.0, r.old_sums[g, rows_of(q), :])
    for i, name in enumerate("axyz"):
        if slot:
            reset = r.column_cluster[i : i + 1, :] <= (0 if slot % 2 else 1)
            getattr(r, "old_" + name)[...] = jnp.where(reset, 0.0, getattr(r, "sum_" + name)[...])
        else:
            getattr(r, "old_" + name)[...] = jnp.zeros((SEND_ROWS, LANES), F32)
    if slot == 3:
        for f in range(FACES):
            lane = r.index[8 + f : 9 + f, :]
            face = r.index[16 + f : 17 + f, :]
            total = None
            for g in range(FACES):
                value = jnp.where(face == g, take_lanes(sums[g], lane), 0.0)
                total = value if total is None else total + value
            r.gathered[f] = total
    if slot == 0:
        fields = [r.taylor[0, q] for q in range(QUANTITIES)]
        steps = [r.step[q] for q in range(QUANTITIES)]
    else:
        fields = [unpacked("fields", q) for q in range(QUANTITIES)]
        steps = [unpacked("step", q) for q in range(QUANTITIES)]
        if slot == 2:
            for q in range(QUANTITIES):
                steps[q] = steps[q] + jnp.where(cluster == 1, unpack_quantity(lambda k: r.second1[k], q, rank), 0.0)
    right = side_by_side([tall_basis(value) for value in steps])
    own = matmul(r.proj_w[...], right)
    apply_flux(r.flux_own, lambda f, p: own[rows_of(f), lanes_of(p)], r.lift_in)
    lifted = lift(r.lift_w, r.lift_in)
    r.work[...] = matmul(r.update_w[...], right)

    def put(q, value):
        value = fields[q] + value - lifted[:BASIS_PAD, lanes_of(q)]
        r.base[q] = value if slot == 0 else jnp.where(started, value, r.old_base[q])

    apply_star(r.star, r.work, put)
    if slot == 1:
        pack_block(r, 1, r.where1, r.star1, r.flux1)
    if slot == 0:
        for j, later in ((1, r.later1), (2, r.later2), (3, r.later3)):

            def store(g, q, value, later=later):
                later[g, rows_of(q), :] = value

            rotated_faces(r.turn_w, r.orientation, [integral(r.taylor, q, j) for q in range(QUANTITIES)], store)
    if slot == 2:

        def merge(g, q, value):
            r.next_later[g, rows_of(q), :] = jnp.where(cluster == 1, value, r.after[g, rows_of(q), :])

        rotated_faces(
            r.turn_w,
            r.orientation,
            [unpack_quantity(lambda k: r.second1[k], q, rank) for q in range(QUANTITIES)],
            merge,
        )
    if slot == 3:
        return
    later = r.later1 if slot == 0 else r.after if slot == 1 else r.next_later
    pack_sends(later, r.send_index, [getattr(r, "later_" + name) for name in NAMES])
    targets = [(r.base0, r.ahead0, r.gathered0, r.where0)]
    if slot == 1:
        targets.append((r.base1, r.ahead1, r.gathered1, r.where1))
    for block, (base, ahead, gathered, where) in enumerate(targets):
        packed = pack_quantities([r.base[q] for q in range(QUANTITIES)], r.packs[block : block + 1, :])
        for k in range(PACKS):
            base[k] = packed[k]
        packed_derivatives(packed, r.deriv_w, ahead)
        lane, face = where[5:6, :], where[6:7, :]
        total = None
        for g in range(FACES):
            value = jnp.where(face == g, take_lanes(sums[g], lane), 0.0)
            total = value if total is None else total + value
        gathered[...] = total


def shape_of(array):
    return jax.ShapeDtypeStruct(array.shape, array.dtype)


def shape(*dims):
    return jax.ShapeDtypeStruct(dims, F32)


def ints(rows):
    return jax.ShapeDtypeStruct((rows, LANES), jnp.int32)


RECEIVED = ("got_a", "got_x", "got_y", "got_z")
TAYLOR = shape(ORDER, QUANTITIES, BASIS_PAD, LANES)
STATE = shape(QUANTITIES, BASIS_PAD, LANES)
PACKED = shape(PACKS, BASIS_PAD, LANES)
AHEAD = shape(LANES, PACKS * LANES)
PACKED_STAR = shape(QUANTITIES, PACKS, 3, LANES)
PACKED_FLUX = shape(QUANTITIES, QUANTITIES, LANES)
PACKED_LIFT = shape(FACES * FACE_PAD, PACKS * LANES)
TURNED = shape(FACES, FACE_ROWS, LANES)
TILE = shape(FACE_ROWS, LANES)
SQUARE = shape(LANES, LANES)
WORK = shape(LANES, QUANTITIES * LANES)
LIFT_IN = shape(FACES * FACE_PAD, QUANTITIES * LANES)
SENDS = {NAMES[i]: shape(SEND_ROWS, LANES) for i in SEND_ORDER}
OLD = {"old_" + name: shape(SEND_ROWS, LANES) for name in "axyz"}
SUMS = {"sum_" + name: shape(SEND_ROWS, LANES) for name in "axyz"}
LATER_SENDS = {"later_" + name: value for name, value in SENDS.items()}
EARLY_FLOPS = 5_000_000_000


def call(kernel, name, ins, outs, scratch, flops):
    names = [*ins, *outs, *scratch]
    size = sum(math.prod(a.shape) * 4 for a in [*ins.values(), *outs.values()])

    def run(*refs):
        kernel(types.SimpleNamespace(**dict(zip(names, refs))))

    result = pl.pallas_call(
        run,
        out_shape=list(outs.values()),
        in_specs=[VMEM] * len(ins),
        out_specs=[VMEM] * len(outs),
        scratch_shapes=[pltpu.VMEM(a.shape, a.dtype) for a in scratch.values()],
        compiler_params=pltpu.CompilerParams(vmem_limit_bytes=32 * 1024 * 1024),
        cost_estimate=pl.CostEstimate(flops=flops, bytes_accessed=size, transcendentals=0),
        name=name,
    )(*ins.values())
    return dict(zip(outs, result))


def some(values, *names):
    return {name: values[name] for name in names}


def body(
    dofs, star, flux_local, flux_neigh, neighbour, neighbour_face, orientation, face_kind, cluster,
    deriv_stiff, update_stiff, face_proj, face_lift, orient_map,
):
    devices = lax.axis_size("dom")
    star, flux_local, flux_neigh = [jnp.transpose(a, (1, 2, 0, 3)) for a in (star, flux_local, flux_neigh)]
    face_proj, face_lift = jnp.transpose(face_proj, (1, 0, 2)), jnp.transpose(face_lift, (2, 0, 1))
    v = dict(
        star=star, flux_local=flux_local, flux_neigh=flux_neigh, neighbour=neighbour,
        face_kind=face_kind, update=update_stiff, lift_mat=face_lift,
    )
    frame = call(frame_kernel, "frame", {}, dict(frame=SQUARE), {}, EARLY_FLOPS)["frame"]
    ready = call(
        functools.partial(prepare_kernel, devices),
        "prepare",
        dict(frame=frame, neighbour=neighbour, neighbour_face=neighbour_face, face_kind=face_kind,
             orientation=orientation, cluster=cluster, deriv=deriv_stiff, proj=face_proj, orient=orient_map),
        dict(deriv_w=SQUARE, far_out=ints(FACES), proj_w=shape(64, LANES), turn_w=shape(192, LANES), send_index=ints(8),
             orientation_out=ints(FACES), cluster_out=ints(1)),
        dict(flip=SQUARE),
        EARLY_FLOPS,
    )
    v.update(ready, orientation=ready["orientation_out"], cluster=ready["cluster_out"], neighbour_face=ready["far_out"])
    sends = call(
        first_kernel,
        "start",
        dict(dofs=dofs, **some(v, "star", "orientation", "cluster", "deriv_w", "turn_w", "send_index")),
        dict(taylor=TAYLOR, step=STATE, faces=TURNED, **SENDS),
        dict(work=WORK, spare=WORK),
        100_000_000,
    )
    receives = exchange(sends)
    kept = call(
        functools.partial(beside_kernel, 0, devices),
        "beside0",
        {**some(sends, "taylor", "step", "faces"),
         **some(v, "star", "orientation", "cluster", "flux_local", "flux_neigh", "face_kind", "neighbour",
                "neighbour_face", "update", "lift_mat", "deriv_w", "proj_w", "turn_w", "send_index")},
        dict(base=STATE, sums=TURNED, source_cluster=ints(FACES), column_cluster=ints(4), **OLD,
             flux_own=shape_of(flux_local), later1=TURNED, later2=TURNED,
             later3=TURNED, update_w=SQUARE, lift_w=shape(176, 256), index=ints(24), packs=ints(8),
             send_packs=ints(12), where0=ints(8), star0=PACKED_STAR, flux0=PACKED_FLUX,
             base0=PACKED, ahead0=AHEAD, gathered0=TILE, **LATER_SENDS),
        dict(work=WORK, lift_in=LIFT_IN, flip=SQUARE),
        50_000_000,
    )
    v.update(kept)
    later = {1: v["later1"], 2: v["later2"], 3: v["later3"]}
    for slot in range(1, SLOTS):
        numbers = (0, 1) if slot == 2 else (0,)
        per_block = [name + str(b) for b in numbers for name in ("base", "ahead", "gathered", "flux", "star", "where")]
        outs, scratch = {}, {}
        for b in numbers:
            outs.update({"fields%d" % b: PACKED, "step%d" % b: PACKED, "faces%d" % b: shape(FACES, 48, LANES)})
            scratch.update(
                {"work%d" % b: AHEAD, "spare%d" % b: AHEAD, "lift_in%d" % b: PACKED_LIFT}
            )
        if slot == 2:
            outs["second1"] = PACKED
        sends = call(
            functools.partial(slot_kernel, slot),
            "slot%d" % slot,
            {**receives, **some(v, *OLD, *per_block, *LATER_SENDS, "deriv_w", "turn_w", "lift_w", "send_packs")},
            {**outs, **SUMS, **SENDS},
            scratch,
            100_000_000,
        )
        receives = exchange(sends)
        ins = some(sends, *outs, *SUMS)
        ins.update(old_base=v["base"], old_sums=v["sums"], later=later[slot])
        ins.update(
            some(v, "star", "cluster", "flux_own", "proj_w", "update_w", "lift_w", "packs", "source_cluster",
                 "column_cluster")
        )
        results = dict(base=STATE, **OLD)
        scratch = dict(work=WORK, lift_in=LIFT_IN)
        if slot < 3:
            ins.update(after=later[slot + 1], **some(v, "send_index", "deriv_w", "where0"))
            results.update(sums=TURNED, base0=PACKED, ahead0=AHEAD, gathered0=TILE, **LATER_SENDS)
        else:
            ins.update(some(v, "index"))
            results.update(gathered=TURNED)
            scratch.update(sums=TURNED)
        if slot == 1:
            ins.update(some(v, "flux_neigh", "orientation", "index"))
            results.update(base1=PACKED, ahead1=AHEAD, gathered1=TILE, where1=ints(8), star1=PACKED_STAR,
                           flux1=PACKED_FLUX)
        if slot == 2:
            ins.update(some(v, "orientation", "turn_w"))
            results.update(next_later=TURNED)
        v.update(
            call(
                functools.partial(beside_kernel, slot, devices), "beside%d" % slot, ins, results,
                scratch, 50_000_000,
            )
        )
        if slot == 2:
            later[3] = v["next_later"]
    return call(
        last_kernel,
        "finish",
        {**receives, **some(v, *OLD, "base", "gathered", "flux_neigh", "lift_w", "index")},
        dict(out=shape(*dofs.shape)),
        dict(**SUMS, near=TILE, far=TILE, collected=TURNED, lift_in=LIFT_IN),
        10_000_000,
    )["out"]


def solution(mesh):
    in_specs = (
        P(None, None, "dom"),
        P(None, None, None, "dom"),
        P(None, None, None, "dom"),
        P(None, None, None, "dom"),
        P(None, "dom"),
        P(None, "dom"),
        P(None, "dom"),
        P(None, "dom"),
        P("dom"),
        P(),
        P(),
        P(),
        P(),
        P(),
    )
    out_specs = P(None, None, "dom")
    return jax.shard_map(body, mesh=mesh, in_specs=in_specs, out_specs=out_specs, check_vma=False)
```

```python
import functools
import math
import types

import jax
import jax.numpy as jnp
from jax import lax
from jax.experimental import pallas as pl
from jax.experimental.pallas import tpu as pltpu
from jax.sharding import PartitionSpec as P

CAP_NEAR = 64
CAP_FAR = 32
QUANTITIES = 9
BASIS = 35
BASIS_PAD = 40
FACE_BASIS = 15
FACE_PAD = 16
FACES = 4
ORDER = 5
SLOTS = 4
LANES = 128
FACE_ROWS = QUANTITIES * FACE_PAD
SEND_ROWS = 80
PACK = 32
GROUPS = LANES // PACK
PACKS = 3

OFFSETS = (1, -1, 2, -2)
SEND_ORDER = (2, 1, 3, 0)
F32 = jnp.float32
BF16 = jnp.bfloat16
VMEM = pl.BlockSpec(memory_space=pltpu.VMEM)
NAMES = ("sent_a", "sent_x", "sent_y", "sent_z")


def exchange(sends):
    devices = lax.axis_size("dom")
    receives = {}
    for partner in SEND_ORDER:
        by = OFFSETS[partner]
        pairs = [(i, (i + (by if i % 2 == 0 else -by)) % devices) for i in range(devices)]
        receives[RECEIVED[partner]] = lax.ppermute(sends[NAMES[partner]], "dom", pairs)
    return receives


def split(x):
    high = x.astype(BF16).astype(F32)
    return high, x - high


def wide_basis(matrix):
    high, low = split(matrix)
    return high + pltpu.roll(high, 40, 1) + pltpu.roll(low, 80, 1)


def tall_basis(x):
    high, low = split(x)
    rest = jnp.zeros((LANES - 3 * BASIS_PAD, x.shape[1]), F32)
    return jnp.concatenate([high, low, high, rest], axis=0).astype(BF16)


def wide_faces(matrix):
    high, low = split(matrix)
    return jnp.concatenate([high + pltpu.roll(high, 64, 1), low], axis=1)


def tall_faces(x):
    high, low = split(x)
    return jnp.concatenate([high, low, high], axis=0).astype(BF16)


def matmul(left, right):
    return jnp.dot(left.astype(BF16), right, preferred_element_type=F32)


def side_by_side(pieces):
    return jnp.concatenate(pieces, axis=1)


def lanes_of(q):
    return slice(q * LANES, (q + 1) * LANES)


def star_tile(star, work, quantities, groups):
    total = [None] * len(quantities)
    for d in range(3):
        for p in range(groups):
            piece = work[d * BASIS_PAD : (d + 1) * BASIS_PAD, lanes_of(p)]
            for i, q in enumerate(quantities):
                term = star[q, p, d : d + 1, :] * piece
                total[i] = term if total[i] is None else total[i] + term
    return total


def apply_star(star, work, put):
    for first in range(0, QUANTITIES, 3):
        for i, value in enumerate(star_tile(star, work, range(first, first + 3), QUANTITIES)):
            put(first + i, value)


def apply_flux(flux, faces, lift_in):
    for f in range(FACES):
        total = [None] * QUANTITIES
        for p in range(QUANTITIES):
            piece = faces(f, p)
            for q in range(QUANTITIES):
                term = flux[q, p, f : f + 1, :] * piece
                total[q] = term if total[q] is None else total[q] + term
        for q in range(QUANTITIES):
            lift_in[f * FACE_PAD : (f + 1) * FACE_PAD, lanes_of(q)] = total[q]


def lift(lift_w, lift_in):
    right = side_by_side([tall_faces(lift_in[:, lanes_of(q)]) for q in range(QUANTITIES)])
    return matmul(lift_w[0:48, :192], right)


def predict(taylor, star, deriv_w, works):
    for k in range(ORDER):
        for first in range(0, QUANTITIES, 3):
            if k:
                values = star_tile(star, works[k % 2], range(first, first + 3), QUANTITIES)
                for i in range(3):
                    taylor[k, first + i] = values[i]
            else:
                values = [taylor[0, first + i] for i in range(3)]
            if k < ORDER - 1:
                right = side_by_side([tall_basis(value) for value in values])
                works[(k + 1) % 2][:, first * LANES : (first + 3) * LANES] = matmul(deriv_w[...], right)


def integral(taylor, q, j):
    total = None
    for k in range(ORDER):
        weight = ((j + 1) ** (k + 1) - j ** (k + 1)) / math.factorial(k + 1)
        term = taylor[k, q] * weight
        total = term if total is None else total + term
    return total


def step_integral(taylor, q, span):
    total = None
    power = span
    for k in range(ORDER):
        term = taylor[k, q] * (power * (1.0 / math.factorial(k + 1)))
        total = term if total is None else total + term
        power = power * span
    return total


def rotated_faces(turn_w, orientation, integrals, put):
    right = side_by_side([tall_basis(value) for value in integrals])
    result = matmul(turn_w[...], right)
    for g in range(FACES):
        turn = orientation[g : g + 1, :]
        for q in range(QUANTITIES):
            parts = []
            for o in range(3):
                first = (o * FACES + g) * FACE_PAD
                parts.append(result[first : first + FACE_PAD, lanes_of(q)])
            put(g, q, jnp.where(turn == 0, parts[0], jnp.where(turn == 1, parts[1], parts[2])))


def rows_of(q):
    return slice(q * FACE_PAD, (q + 1) * FACE_PAD)


def take_lanes(source, index):
    if source.shape[0] == 1:
        return take_lanes(jnp.broadcast_to(source, (8, LANES)), index)[0:1, :]
    return jnp.take_along_axis(source, jnp.broadcast_to(index, source.shape), axis=1)


def turn_lanes(x, shift):
    return pltpu.roll(x, shift % LANES, 1) if shift % LANES else x


def choose(pieces, lane, width):
    total = pieces[0]
    for j in range(1, len(pieces)):
        total = jnp.where(lane // width == j, pieces[j], total)
    return total


def pack_sends(faces, index, sends):
    tiles = []
    for row in (0, 2):
        lane = index[row : row + 1, :]
        face = index[row + 1 : row + 2, :]
        tile = take_lanes(faces[0], lane)
        for g in range(1, FACES):
            tile = jnp.where(face == g, take_lanes(faces[g], lane), tile)
        tiles.append(tile)
    lane = lax.broadcasted_iota(jnp.int32, (FACE_PAD, LANES), 1)
    nothing = jnp.zeros((FACE_PAD, LANES), F32)

    def piece(tile, q):
        return tiles[tile][rows_of(q), :] if q < QUANTITIES else nothing

    for k in range(5):
        low, high = piece(0, 2 * k), piece(0, 2 * k + 1)
        sends[0][rows_of(k), :] = choose([low, turn_lanes(high, 64)], lane, 64)
        sends[1][rows_of(k), :] = choose([turn_lanes(low, 64), high], lane, 64)
    for k in range(5):
        for side in range(2):
            value = nothing
            if k < PACKS:
                parts = [turn_lanes(piece(1, 4 * k + j), 32 * j - 64 * side) for j in range(4)]
                value = choose(parts, lane, 32)
            sends[2 + side][rows_of(k), :] = value


def unpack_receives(receives, near, far):
    lane = lax.broadcasted_iota(jnp.int32, (FACE_PAD, LANES), 1)
    for q in range(QUANTITIES):
        ahead, behind = receives[0][rows_of(q // 2), :], receives[1][rows_of(q // 2), :]
        shift = 64 * (q % 2)
        near[rows_of(q), :] = choose([turn_lanes(ahead, shift), turn_lanes(behind, 64 + shift)], lane, 64)
        ahead, behind = receives[2][rows_of(q // 4), :], receives[3][rows_of(q // 4), :]
        shift = -32 * (q % 4)
        far[rows_of(q), :] = choose([turn_lanes(ahead, shift), turn_lanes(behind, 64 + shift)], lane, 64)


def add_remote(index, near, far, collected, put):
    for f in range(FACES):
        place = index[f : f + 1, :]
        lane = jnp.bitwise_and(place, LANES - 1)
        from_near = take_lanes(near[...], lane)
        from_far = take_lanes(far[...], lane)
        remote = jnp.where(place >= LANES, from_far, jnp.where(place >= 0, from_near, 0.0))
        put(f, collected[f] + remote)


def transposed(rows, flip):
    flip[...] = jnp.zeros((LANES, LANES), F32)
    for f in range(FACES):
        flip[f : f + 1, :] = rows[f]
    return flip[...].T


def ranks(keys, flip):
    columns = transposed(keys, flip)
    result = []
    for f in range(FACES):
        total = None
        for other in range(FACES):
            less = jnp.where(columns[:, other : other + 1] < keys[f], 1.0, 0.0)
            total = less if total is None else total + less
        result.append(jnp.sum(total, axis=0, keepdims=True))
    return result


def group_places(groups, keys, flip):
    bases = (0.0, 64.0, 128.0, 192.0)
    order = ranks([groups[f] * 512.0 + keys[f] for f in range(FACES)], flip)
    sizes = []
    for partner in range(FACES):
        total = None
        for f in range(FACES):
            here = jnp.where(groups[f] == partner, 1.0, 0.0)
            total = here if total is None else total + here
        sizes.append(jnp.sum(total, axis=1, keepdims=True))
    places = []
    for f in range(FACES):
        place = jnp.full((1, LANES), -1.0, F32)
        start = jnp.zeros((1, 1), F32)
        for partner in range(FACES):
            place = jnp.where(groups[f] == partner, order[f] - start + bases[partner], place)
            start = start + sizes[partner]
        places.append(place)
    return places


def partner_groups(devices, neighbour, face_kind):
    here = lax.axis_index("dom")
    sign = 1 - 2 * jnp.bitwise_and(here, 1)
    targets = [jnp.where(sign * by < 0, sign * by + devices, sign * by) for by in OFFSETS]
    sources = targets[:2] + [devices - far for far in targets[2:]]
    send_groups, recv_groups, local = [], [], []
    for f in range(FACES):
        interior = face_kind[f : f + 1, :] == 0
        distance = lax.shift_right_logical(neighbour[f : f + 1, :], 7) - here
        distance = jnp.where(distance < 0, distance + devices, distance)
        send = jnp.full((1, LANES), 4, jnp.int32)
        recv = jnp.full((1, LANES), 4, jnp.int32)
        for partner in range(4):
            send = jnp.where(interior & (distance == targets[partner]), partner, send)
            recv = jnp.where(interior & (distance == sources[partner]), partner, recv)
        send_groups.append(send.astype(F32))
        recv_groups.append(recv.astype(F32))
        local.append(interior & (distance == 0))
    return send_groups, recv_groups, local


def make_send_index(devices, neighbour, face_kind, index, flip):
    groups, _, _ = partner_groups(devices, neighbour, face_kind)
    element = lax.broadcasted_iota(jnp.int32, (1, LANES), 1)
    keys = [(element + f * LANES).astype(F32) for f in range(FACES)]
    places = group_places(groups, keys, flip)
    for tile, (element, face) in enumerate(columns_of(places, flip)):
        index[2 * tile : 2 * tile + 1, :] = element
        index[2 * tile + 1 : 2 * tile + 2, :] = face


def columns_of(places, flip):
    columns = transposed(places, flip)
    row = lax.broadcasted_iota(jnp.int32, (LANES, LANES), 0).astype(F32)
    lane = lax.broadcasted_iota(jnp.int32, (LANES, LANES), 1).astype(F32)
    result = []
    for tile in range(2):
        total = None
        for f in range(FACES):
            hit = jnp.where(columns[:, f : f + 1] == lane + tile * 128.0, row + f * 128.0, 0.0)
            total = hit if total is None else total + hit
        code = jnp.sum(total, axis=0, keepdims=True).astype(jnp.int32)
        result.append((jnp.bitwise_and(code, LANES - 1), lax.shift_right_logical(code, 7)))
    return result


def make_recv_index(devices, neighbour, neighbour_face, face_kind, index, flip):
    _, groups, local = partner_groups(devices, neighbour, face_kind)
    index[...] = jnp.zeros((24, LANES), jnp.int32)
    keys = []
    for f in range(FACES):
        far_face = neighbour_face[f : f + 1, :]
        far_element = jnp.bitwise_and(neighbour[f : f + 1, :], LANES - 1)
        keys.append((far_face * LANES + far_element).astype(F32))
        index[8 + f : 9 + f, :] = far_element
        index[16 + f : 17 + f, :] = jnp.where(local[f], far_face, -1)
    places = group_places(groups, keys, flip)
    for f in range(FACES):
        index[f : f + 1, :] = places[f].astype(jnp.int32)


def make_deriv(deriv, frame, deriv_w):
    deriv_w[...] = frame[...]
    for d in range(3):
        deriv_w[d * BASIS_PAD : d * BASIS_PAD + BASIS, :BASIS] = -deriv[d]
    deriv_w[...] = wide_basis(deriv_w[...])


def make_faces(proj, orient, frame, proj_w, turn_w, flip):
    proj_w[...] = frame[0:64, :]
    for g in range(FACES):
        proj_w[g * FACE_PAD : g * FACE_PAD + FACE_BASIS, :BASIS] = proj[:, g, :]
    right = side_by_side([proj_w[rows_of(g), :] for g in range(FACES)])
    flip[...] = frame[...]
    for o in range(3):
        flip[o * FACE_PAD : o * FACE_PAD + FACE_BASIS, :FACE_BASIS] = orient[o]
    turned = jnp.dot(
        flip[0:48, :FACE_PAD], right, precision=lax.Precision.HIGHEST, preferred_element_type=F32
    )
    for o in range(3):
        for g in range(FACES):
            turn_w[rows_of(o * FACES + g), :] = wide_basis(turned[rows_of(o), lanes_of(g)])
    proj_w[...] = wide_basis(proj_w[...])


def make_update(update, update_w, flip):
    update_w[...] = jnp.zeros((LANES, LANES), F32)
    for d in range(3):
        flip[...] = jnp.zeros((LANES, LANES), F32)
        flip[:BASIS, :BASIS] = update[d]
        update_w[d * BASIS_PAD : (d + 1) * BASIS_PAD, :] = flip[...].T[:BASIS_PAD, :]
    update_w[...] = wide_basis(update_w[...])


def make_lift(lift_mat, deriv_w, lift_w, flip):
    total = None
    for f in range(FACES):
        flip[...] = jnp.zeros((LANES, LANES), F32)
        flip[:FACE_BASIS, :BASIS] = lift_mat[:, f, :]
        value = turn_lanes(flip[...].T[0:48, :], 16 * f)
        total = value if total is None else total + value
    lift_w[0:48, :] = wide_faces(total)
    lift_w[48:176, :] = wide_faces(matmul(deriv_w[...], tall_basis(total[0:BASIS_PAD, :])))


def pack(pieces, element, lane):
    return choose([take_lanes(piece, element) for piece in pieces], lane, PACK)


def pack_quantities(pieces, element):
    lane = lax.broadcasted_iota(jnp.int32, pieces[0].shape, 1)
    nothing = jnp.zeros(pieces[0].shape, F32)
    result = []
    for k in range(PACKS):
        group = [take_lanes(pieces[q], element) if q < QUANTITIES else nothing for q in range(4 * k, 4 * k + 4)]
        result.append(choose(group, lane, PACK))
    return result


def unpack_quantity(packed, q, rank):
    return take_lanes(packed(q // 4), rank + PACK * (q % 4))


def make_packs(r):
    row = lax.broadcasted_iota(jnp.int32, (LANES, LANES), 0).astype(F32)
    lane = lax.broadcasted_iota(jnp.int32, (LANES, LANES), 1)
    cluster = r.cluster[...].astype(F32)
    columns = transposed([cluster] * FACES, r.flip)
    before = jnp.where((columns[:, 0:1] == cluster) & (row < lane.astype(F32)), 1.0, 0.0)
    rank = jnp.sum(before, axis=0, keepdims=True)
    columns = transposed([cluster * 64.0 + rank] * FACES, r.flip)
    r.packs[...] = jnp.zeros((8, LANES), jnp.int32)
    for block in range(2):
        wanted = jnp.bitwise_and(lane, PACK - 1).astype(F32) + 64.0 * block
        hit = jnp.where(columns[:, 0:1] == wanted, row, 0.0)
        r.packs[block : block + 1, :] = jnp.sum(hit, axis=0, keepdims=True).astype(jnp.int32)
    rank = rank.astype(jnp.int32)
    r.packs[2:3, :] = jnp.bitwise_and(rank, PACK - 1)
    lane = lax.broadcasted_iota(jnp.int32, (1, LANES), 1)
    kinds = r.cluster[...]
    for f in range(FACES):
        r.source_cluster[f : f + 1, :] = take_lanes(kinds, r.index[8 + f : 9 + f, :])
    got = [r.index[f : f + 1, :].astype(F32) for f in range(FACES)]
    for tile, (element, _) in enumerate(columns_of(got, r.flip)):
        kind = take_lanes(kinds, element)
        for side in range(2):
            width = 32 if tile else 64
            parts = [turn_lanes(kind, width * j - 64 * side) for j in range(LANES // width)]
            first = 2 * tile + side
            r.column_cluster[first : first + 1, :] = choose(parts, lane, width)
    for tile in range(2):
        element = r.send_index[2 * tile : 2 * tile + 1, :]
        face = r.send_index[2 * tile + 1 : 2 * tile + 2, :]
        kind = take_lanes(kinds, element)
        order = take_lanes(jnp.bitwise_and(rank, PACK - 1), element)
        rows = [order] + [jnp.where(kind == block, face, -1) for block in range(2)]
        for side in range(2):
            width = 32 if tile else 64
            for i in range(3):
                parts = [turn_lanes(rows[i], width * j - 64 * side) for j in range(LANES // width)]
                value = choose(parts, lane, width)
                if i == 0:
                    value = value + PACK * (lane // width)
                first = 3 * (2 * tile + side) + i
                r.send_packs[first : first + 1, :] = value


def pack_flux(flux, element, packed):
    lane = lax.broadcasted_iota(jnp.int32, (FACES, LANES), 1)
    face = lax.broadcasted_iota(jnp.int32, (FACES, LANES), 0)
    for q in range(QUANTITIES):
        for p in range(QUANTITIES):
            value = jnp.where(face == lane // PACK, take_lanes(flux[q, p], element), 0.0)
            packed[q, p : p + 1, :] = jnp.sum(value, axis=0, keepdims=True)


def pack_block(r, block, where, star, flux):
    element = r.packs[block : block + 1, :]
    lane = lax.broadcasted_iota(jnp.int32, (1, LANES), 1)
    where[...] = jnp.zeros((8, LANES), jnp.int32)
    where[0:1, :] = pack([r.index[f : f + 1, :] for f in range(FACES)], element, lane)
    where[1:5, :] = take_lanes(r.orientation[...], element)
    where[5:6, :] = pack([r.index[8 + f : 9 + f, :] for f in range(FACES)], element, lane)
    where[6:7, :] = pack([r.index[16 + f : 17 + f, :] for f in range(FACES)], element, lane)
    for q in range(QUANTITIES):
        for k, value in enumerate(pack_quantities([r.star[q, p] for p in range(QUANTITIES)], element)):
            star[q, k] = value
    pack_flux(r.flux_neigh, element, flux)


def spread_faces(total, lift_in):
    lane = lax.broadcasted_iota(jnp.int32, (FACE_PAD, LANES), 1)
    nothing = jnp.zeros((FACE_PAD, LANES), F32)
    for k in range(PACKS):
        for f in range(FACES):
            parts = []
            for j in range(GROUPS):
                q = GROUPS * k + j
                parts.append(turn_lanes(total[q], PACK * (j - f)) if q < QUANTITIES else nothing)
            lift_in[f * FACE_PAD : (f + 1) * FACE_PAD, lanes_of(k)] = choose(parts, lane, PACK)
    return side_by_side([tall_faces(lift_in[:, lanes_of(k)]) for k in range(PACKS)])


def packed_fields(r, block, base, ahead, gathered, flux, where, lift_in, work):
    near_refs = (r.got_a, r.got_x) if block == 0 else (r.sum_a, r.sum_x)
    far_refs = (r.got_y, r.got_z) if block == 0 else (r.sum_y, r.sum_z)
    place = where[0:1, :]
    near = jnp.bitwise_and(place, 63)
    far = jnp.bitwise_and(place, PACK - 1)
    total = [None] * QUANTITIES
    for p in range(QUANTITIES):
        got = [take_lanes(ref[rows_of(p // 2), :], near + 64 * (p % 2)) for ref in near_refs]
        got += [take_lanes(ref[rows_of(p // 4), :], far + PACK * (p % 4)) for ref in far_refs]
        remote = jnp.where(place < 64, got[0], jnp.where(place < 128, got[1], jnp.where(place < 192, got[2], got[3])))
        piece = gathered[rows_of(p), :] + jnp.where(place >= 0, remote, 0.0)
        for q in range(QUANTITIES):
            term = flux[q, p : p + 1, :] * piece
            total[q] = term if total[q] is None else total[q] + term
    right = spread_faces(total, lift_in)
    lifted = matmul(r.lift_w[:, :192], right)
    work[...] = ahead[...] - lifted[48:176, :]
    return [base[k] - lifted[:BASIS_PAD, lanes_of(k)] for k in range(PACKS)]


def packed_derivatives(terms, deriv_w, work):
    for k in range(PACKS):
        work[:, lanes_of(k)] = matmul(deriv_w[...], tall_basis(terms[k]))


def gather_copies(values):
    lane = lax.broadcasted_iota(jnp.int32, (BASIS_PAD, LANES), 1)
    if len(values) == 1:
        total = values[0] + pltpu.roll(values[0], 64, 1)
        return jnp.where(lane < PACK, total + pltpu.roll(total, 96, 1), 0.0)
    low = lane < 64
    halves = []
    for i in range(2):
        a, b = values[i], values[i + 2]
        halves.append(jnp.where(low, a, b) + pltpu.roll(jnp.where(low, b, a), 64, 1))
    even = jnp.bitwise_and(lane, PACK) == 0
    swapped = take_lanes(jnp.where(even, halves[1], halves[0]), jnp.bitwise_xor(lane[0:1, :], PACK))
    return jnp.where(even, halves[0], halves[1]) + swapped


def packed_star(star, work, follow=None):
    result = []
    for k in range(PACKS):
        quantities = range(GROUPS * k, min(GROUPS * (k + 1), QUANTITIES))
        result.append(gather_copies(star_tile(star, work, quantities, PACKS)))
        if follow is not None:
            follow(k, result[k])
    return result


def packed_faces(integrals, turn_w, where, put):
    right = side_by_side([tall_basis(value) for value in integrals])
    result = matmul(turn_w[...], right)
    for g in range(FACES):
        turn = where[1 + g : 2 + g, :]
        for k in range(PACKS):
            parts = [result[rows_of(o * FACES + g), lanes_of(k)] for o in range(3)]
            put(g, k, jnp.where(turn == 0, parts[0], jnp.where(turn == 1, parts[1], parts[2])))


def add_terms(total, terms, weight):
    values = [term * weight for term in terms]
    return values if total is None else [a + b for a, b in zip(total, values)]


def add_received(r):
    for name in "axyz":
        getattr(r, "sum_" + name)[...] = getattr(r, "got_" + name)[...] + getattr(r, "old_" + name)[...]


def slot_kernel(slot, r):
    if slot == 2:
        add_received(r)
    numbers = (0, 1) if slot == 2 else (0,)
    names = ("base", "ahead", "gathered", "flux", "where", "lift_in", "star", "fields", "step", "faces", "work", "spare")
    blocks = [types.SimpleNamespace(**{name: getattr(r, name + str(b)) for name in names}) for b in numbers]
    terms = []
    for b, block in enumerate(blocks):
        terms.append(
            packed_fields(
                r, b, block.base, block.ahead, block.gathered, block.flux, block.where, block.lift_in, block.work
            )
        )
        for k in range(PACKS):
            block.fields[k] = terms[-1][k]
    first = [None] * len(blocks)
    second = None
    for k in range(ORDER):
        for b, block in enumerate(blocks):
            if k:
                work, other = (block.work, block.spare) if k % 2 else (block.spare, block.work)

                def follow(i, value, other=other):
                    other[:, lanes_of(i)] = matmul(r.deriv_w[...], tall_basis(value))

                terms[b] = packed_star(block.star, work, follow if k < ORDER - 1 else None)
            first[b] = add_terms(first[b], terms[b], 1.0 / math.factorial(k + 1))
        if slot == 2:
            second = add_terms(second, terms[1], (2.0 ** (k + 1) - 1.0) / math.factorial(k + 1))
    for b, block in enumerate(blocks):

        def put(g, k, value, faces=block.faces):
            faces[g, rows_of(k), :] = value

        packed_faces(first[b], r.turn_w, block.where, put)
        for k in range(PACKS):
            block.step[k] = first[b][k]
    if slot == 2:
        for k in range(PACKS):
            r.second1[k] = second[k]
    for partner in SEND_ORDER:
        later, sent = getattr(r, "later_" + NAMES[partner]), getattr(r, NAMES[partner])
        near = partner < 2
        lane = r.send_packs[3 * partner : 3 * partner + 1, :]
        for k in range(5 if near else PACKS):
            value = later[rows_of(k), :]
            source = k // 2 if near else k
            place = lane + 64 * (k % 2) if near else lane
            for b, block in enumerate(blocks):
                face = r.send_packs[3 * partner + 1 + b : 3 * partner + 2 + b, :]
                for g in range(FACES):
                    value = jnp.where(face == g, take_lanes(block.faces[g, rows_of(source), :], place), value)
            sent[rows_of(k), :] = value
        if not near:
            sent[48:80, :] = jnp.zeros((32, LANES), F32)


def frame_kernel(r):
    r.frame[...] = jnp.zeros((LANES, LANES), F32)


def first_kernel(devices, r):
    make_deriv(r.deriv, r.frame, r.deriv_w)
    for q in range(QUANTITIES):
        r.taylor[0, q] = jnp.zeros((BASIS_PAD, LANES), F32)
        r.taylor[0, q, :BASIS, :] = r.dofs[q]
    r.orientation_out[...] = r.orientation[...]
    r.cluster_out[...] = r.cluster[...].reshape(1, LANES)
    r.far_out[...] = r.neighbour_face[...]
    make_send_index(devices, r.neighbour, r.face_kind, r.send_index, r.flip)
    make_faces(r.proj, r.orient, r.frame, r.proj_w, r.turn_w, r.flop)
    predict(r.taylor, r.star, r.deriv_w, (r.spare, r.work))
    span = lax.shift_left(jnp.ones_like(r.cluster_out[...]), r.cluster_out[...]).astype(F32)
    for q in range(QUANTITIES):
        r.step[q] = step_integral(r.taylor, q, span)

    def put(g, q, value):
        r.faces[g, rows_of(q), :] = value

    rotated_faces(r.turn_w, r.orientation, [integral(r.taylor, q, 0) for q in range(QUANTITIES)], put)
    pack_sends(r.faces, r.send_index, [getattr(r, name) for name in NAMES])


def last_kernel(r):
    add_received(r)
    unpack_receives([r.sum_a, r.sum_x, r.sum_y, r.sum_z], r.near, r.far)

    def keep(f, value):
        r.collected[f] = value

    add_remote(r.index, r.near, r.far, r.gathered, keep)
    apply_flux(r.flux_neigh, lambda f, p: r.collected[f, rows_of(p), :], r.lift_in)
    lifted = lift(r.lift_w, r.lift_in)
    for q in range(QUANTITIES):
        r.out[q] = (r.base[q] - lifted[:BASIS_PAD, lanes_of(q)])[:BASIS, :]


def later_faces(r, j, later):
    def store(g, q, value):
        later[g, rows_of(q), :] = value

    rotated_faces(r.turn_w, r.orientation, [integral(r.taylor, q, j) for q in range(QUANTITIES)], store)


def beside_kernel(slot, devices, r):
    if slot == 0:
        make_update(r.update, r.update_w, r.flip)
        make_lift(r.lift_mat, r.deriv_w, r.lift_w, r.flip)
        make_recv_index(devices, r.neighbour, r.neighbour_face, r.face_kind, r.index, r.flip)
        make_packs(r)
        pack_block(r, 0, r.where0, r.star0, r.flux0)
        mirror = jnp.where(r.face_kind[...] == 1, 1.0, 0.0)
        for p in range(QUANTITIES):
            sign = -mirror if p < 6 else mirror
            for q in range(QUANTITIES):
                r.flux_own[q, p] = r.flux_local[q, p] + sign * r.flux_neigh[q, p]
    cluster = r.cluster[...]
    started = cluster <= (0 if slot % 2 else 1)
    rank = r.packs[2:3, :]

    def unpacked(name, q, rows=None):
        def packed(ref):
            return (lambda k: ref[k]) if rows is None else (lambda k: ref[rows, rows_of(k), :])

        value = unpack_quantity(packed(getattr(r, name + "0")), q, rank)
        if slot == 2:
            value = jnp.where(cluster == 1, unpack_quantity(packed(getattr(r, name + "1")), q, rank), value)
        return value

    sums = r.sums
    for g in range(FACES):
        reset = r.source_cluster[g : g + 1, :] <= (0 if slot % 2 else 1)
        for q in range(QUANTITIES):
            if slot == 0:
                sums[g, rows_of(q), :] = r.faces[g, rows_of(q), :]
                continue
            value = jnp.where(started, unpacked("faces", q, g), r.later[g, rows_of(q), :])
            sums[g, rows_of(q), :] = value + jnp.where(reset, 0.0, r.old_sums[g, rows_of(q), :])
    if slot:
        for i, name in enumerate("axyz"):
            reset = r.column_cluster[i : i + 1, :] <= (0 if slot % 2 else 1)
            total = getattr(r, "sum_" + name)[...] if slot == 2 else getattr(r, "got_" + name)[...]
            if slot == 3:
                total = total + getattr(r, "older_" + name)[...]
            getattr(r, "old_" + name)[...] = jnp.where(reset, 0.0, total)
    if slot == 3:
        for f in range(FACES):
            lane = r.index[8 + f : 9 + f, :]
            face = r.index[16 + f : 17 + f, :]
            total = None
            for g in range(FACES):
                value = jnp.where(face == g, take_lanes(sums[g], lane), 0.0)
                total = value if total is None else total + value
            r.gathered[f] = total
    if slot == 0:
        fields = [r.taylor[0, q] for q in range(QUANTITIES)]
        steps = [r.step[q] for q in range(QUANTITIES)]
    else:
        fields = [unpacked("fields", q) for q in range(QUANTITIES)]
        steps = [unpacked("step", q) for q in range(QUANTITIES)]
        if slot == 2:
            for q in range(QUANTITIES):
                steps[q] = steps[q] + jnp.where(cluster == 1, unpack_quantity(lambda k: r.second1[k], q, rank), 0.0)
    right = side_by_side([tall_basis(value) for value in steps])
    own = matmul(r.proj_w[...], right)
    apply_flux(r.flux_own, lambda f, p: own[rows_of(f), lanes_of(p)], r.lift_in)
    lifted = lift(r.lift_w, r.lift_in)
    r.work[...] = matmul(r.update_w[...], right)

    def put(q, value):
        value = fields[q] + value - lifted[:BASIS_PAD, lanes_of(q)]
        r.base[q] = value if slot == 0 else jnp.where(started, value, r.old_base[q])

    apply_star(r.star, r.work, put)
    if slot == 1:
        pack_block(r, 1, r.where1, r.star1, r.flux1)
    if slot == 0:
        later_faces(r, 1, r.later1)
    if slot == 1:
        later_faces(r, 2, r.later2)
        later_faces(r, 3, r.later3)
    if slot == 2:

        def merge(g, q, value):
            r.next_later[g, rows_of(q), :] = jnp.where(cluster == 1, value, r.after[g, rows_of(q), :])

        rotated_faces(
            r.turn_w,
            r.orientation,
            [unpack_quantity(lambda k: r.second1[k], q, rank) for q in range(QUANTITIES)],
            merge,
        )
    if slot == 3:
        return
    later = r.later1 if slot == 0 else r.later2 if slot == 1 else r.next_later
    pack_sends(later, r.send_index, [getattr(r, "later_" + name) for name in NAMES])
    targets = [(r.base0, r.ahead0, r.gathered0, r.where0)]
    if slot == 1:
        targets.append((r.base1, r.ahead1, r.gathered1, r.where1))
    for block, (base, ahead, gathered, where) in enumerate(targets):
        packed = pack_quantities([r.base[q] for q in range(QUANTITIES)], r.packs[block : block + 1, :])
        for k in range(PACKS):
            base[k] = packed[k]
        packed_derivatives(packed, r.deriv_w, ahead)
        lane, face = where[5:6, :], where[6:7, :]
        total = None
        for g in range(FACES):
            value = jnp.where(face == g, take_lanes(sums[g], lane), 0.0)
            total = value if total is None else total + value
        gathered[...] = total


def shape_of(array):
    return jax.ShapeDtypeStruct(array.shape, array.dtype)


def shape(*dims):
    return jax.ShapeDtypeStruct(dims, F32)


def ints(rows):
    return jax.ShapeDtypeStruct((rows, LANES), jnp.int32)


RECEIVED = ("got_a", "got_x", "got_y", "got_z")
TAYLOR = shape(ORDER, QUANTITIES, BASIS_PAD, LANES)
STATE = shape(QUANTITIES, BASIS_PAD, LANES)
PACKED = shape(PACKS, BASIS_PAD, LANES)
AHEAD = shape(LANES, PACKS * LANES)
PACKED_STAR = shape(QUANTITIES, PACKS, 3, LANES)
PACKED_FLUX = shape(QUANTITIES, QUANTITIES, LANES)
PACKED_LIFT = shape(FACES * FACE_PAD, PACKS * LANES)
TURNED = shape(FACES, FACE_ROWS, LANES)
TILE = shape(FACE_ROWS, LANES)
SQUARE = shape(LANES, LANES)
WORK = shape(LANES, QUANTITIES * LANES)
LIFT_IN = shape(FACES * FACE_PAD, QUANTITIES * LANES)
SENDS = {NAMES[i]: shape(SEND_ROWS, LANES) for i in SEND_ORDER}
OLD = {"old_" + name: shape(SEND_ROWS, LANES) for name in "axyz"}
SUMS = {"sum_" + name: shape(SEND_ROWS, LANES) for name in "axyz"}
LATER_SENDS = {"later_" + name: value for name, value in SENDS.items()}
EARLY_FLOPS = 5_000_000_000


def call(kernel, name, ins, outs, scratch, flops):
    names = [*ins, *outs, *scratch]
    size = sum(math.prod(a.shape) * 4 for a in [*ins.values(), *outs.values()])

    def run(*refs):
        kernel(types.SimpleNamespace(**dict(zip(names, refs))))

    result = pl.pallas_call(
        run,
        out_shape=list(outs.values()),
        in_specs=[VMEM] * len(ins),
        out_specs=[VMEM] * len(outs),
        scratch_shapes=[pltpu.VMEM(a.shape, a.dtype) for a in scratch.values()],
        compiler_params=pltpu.CompilerParams(vmem_limit_bytes=32 * 1024 * 1024),
        cost_estimate=pl.CostEstimate(flops=flops, bytes_accessed=size, transcendentals=0),
        name=name,
    )(*ins.values())
    return dict(zip(outs, result))


def some(values, *names):
    return {name: values[name] for name in names}


def body(
    dofs, star, flux_local, flux_neigh, neighbour, neighbour_face, orientation, face_kind, cluster,
    deriv_stiff, update_stiff, face_proj, face_lift, orient_map,
):
    devices = lax.axis_size("dom")
    star, flux_local, flux_neigh = [jnp.transpose(a, (1, 2, 0, 3)) for a in (star, flux_local, flux_neigh)]
    face_proj, face_lift = jnp.transpose(face_proj, (1, 0, 2)), jnp.transpose(face_lift, (2, 0, 1))
    v = dict(
        star=star, flux_local=flux_local, flux_neigh=flux_neigh, neighbour=neighbour,
        face_kind=face_kind, update=update_stiff, lift_mat=face_lift,
    )
    frame = call(frame_kernel, "frame", {}, dict(frame=SQUARE), {}, EARLY_FLOPS)["frame"]
    sends = call(
        functools.partial(first_kernel, devices),
        "start",
        dict(frame=frame, neighbour=neighbour, neighbour_face=neighbour_face, face_kind=face_kind,
             orientation=orientation, cluster=cluster, deriv=deriv_stiff, proj=face_proj, orient=orient_map,
             dofs=dofs, star=star),
        dict(deriv_w=SQUARE, far_out=ints(FACES), proj_w=shape(64, LANES), turn_w=shape(192, LANES),
             send_index=ints(8), orientation_out=ints(FACES), cluster_out=ints(1),
             taylor=TAYLOR, step=STATE, faces=TURNED, **SENDS),
        dict(work=WORK, spare=WORK, flip=SQUARE, flop=SQUARE),
        100_000_000,
    )
    v.update(some(sends, "deriv_w", "proj_w", "turn_w", "send_index"), orientation=sends["orientation_out"],
             cluster=sends["cluster_out"], neighbour_face=sends["far_out"])
    receives = exchange(sends)
    kept = call(
        functools.partial(beside_kernel, 0, devices),
        "beside0",
        {**some(sends, "taylor", "step", "faces"),
         **some(v, "star", "orientation", "cluster", "flux_local", "flux_neigh", "face_kind", "neighbour",
                "neighbour_face", "update", "lift_mat", "deriv_w", "proj_w", "turn_w", "send_index")},
        dict(base=STATE, sums=TURNED, source_cluster=ints(FACES), column_cluster=ints(4),
             flux_own=shape_of(flux_local), later1=TURNED, update_w=SQUARE, lift_w=shape(176, 256), index=ints(24), packs=ints(8),
             send_packs=ints(12), where0=ints(8), star0=PACKED_STAR, flux0=PACKED_FLUX,
             base0=PACKED, ahead0=AHEAD, gathered0=TILE, **LATER_SENDS),
        dict(work=WORK, lift_in=LIFT_IN, flip=SQUARE),
        50_000_000,
    )
    v.update(kept)
    v.update(taylor=sends["taylor"])
    for slot in range(1, SLOTS):
        numbers = (0, 1) if slot == 2 else (0,)
        per_block = [name + str(b) for b in numbers for name in ("base", "ahead", "gathered", "flux", "star", "where")]
        outs, scratch = {}, {}
        for b in numbers:
            outs.update({"fields%d" % b: PACKED, "step%d" % b: PACKED, "faces%d" % b: shape(FACES, 48, LANES)})
            scratch.update(
                {"work%d" % b: AHEAD, "spare%d" % b: AHEAD, "lift_in%d" % b: PACKED_LIFT}
            )
        if slot == 2:
            outs["second1"] = PACKED
        sends = call(
            functools.partial(slot_kernel, slot),
            "slot%d" % slot,
            {**receives, **(some(v, *OLD) if slot == 2 else {}),
             **some(v, *per_block, *LATER_SENDS, "deriv_w", "turn_w", "lift_w", "send_packs")},
            {**outs, **(SUMS if slot == 2 else {}), **SENDS},
            scratch,
            100_000_000,
        )
        previous, receives = receives, exchange(sends)
        ins = some(sends, *outs, *(SUMS if slot == 2 else ()))
        if slot != 2:
            ins.update(previous)
        if slot == 3:
            ins.update({"older_" + name: v["old_" + name] for name in "axyz"})
        ins.update(old_base=v["base"], old_sums=v["sums"], later=v["later%d" % slot])
        ins.update(
            some(v, "star", "cluster", "flux_own", "proj_w", "update_w", "lift_w", "packs", "source_cluster",
                 "column_cluster")
        )
        results = dict(base=STATE, **OLD)
        scratch = dict(work=WORK, lift_in=LIFT_IN)
        if slot < 3:
            ins.update(some(v, "send_index", "deriv_w", "where0"))
            results.update(sums=TURNED, base0=PACKED, ahead0=AHEAD, gathered0=TILE, **LATER_SENDS)
        else:
            ins.update(some(v, "index"))
            results.update(gathered=TURNED)
            scratch.update(sums=TURNED)
        if slot == 1:
            ins.update(some(v, "flux_neigh", "orientation", "index", "turn_w", "taylor"))
            results.update(later2=TURNED, later3=TURNED, base1=PACKED, ahead1=AHEAD, gathered1=TILE, where1=ints(8), star1=PACKED_STAR,
                           flux1=PACKED_FLUX)
        if slot == 2:
            ins.update(after=v["later3"], **some(v, "orientation", "turn_w"))
            results.update(next_later=TURNED)
        v.update(
            call(
                functools.partial(beside_kernel, slot, devices), "beside%d" % slot, ins, results,
                scratch, 50_000_000,
            )
        )
        if slot == 2:
            v["later3"] = v["next_later"]
    return call(
        last_kernel,
        "finish",
        {**receives, **some(v, *OLD, "base", "gathered", "flux_neigh", "lift_w", "index")},
        dict(out=shape(*dofs.shape)),
        dict(**SUMS, near=TILE, far=TILE, collected=TURNED, lift_in=LIFT_IN),
        10_000_000,
    )["out"]


def solution(mesh):
    in_specs = (
        P(None, None, "dom"),
        P(None, None, None, "dom"),
        P(None, None, None, "dom"),
        P(None, None, None, "dom"),
        P(None, "dom"),
        P(None, "dom"),
        P(None, "dom"),
        P(None, "dom"),
        P("dom"),
        P(),
        P(),
        P(),
        P(),
        P(),
    )
    out_specs = P(None, None, "dom")
    return jax.shard_map(body, mesh=mesh, in_specs=in_specs, out_specs=out_specs, check_vma=False)
```

```python
import functools
import math
import types

import jax
import jax.numpy as jnp
from jax import lax
from jax.experimental import pallas as pl
from jax.experimental.pallas import tpu as pltpu
from jax.sharding import PartitionSpec as P

CAP_NEAR = 64
CAP_FAR = 32
QUANTITIES = 9
BASIS = 35
BASIS_PAD = 40
FACE_BASIS = 15
FACE_PAD = 16
FACES = 4
ORDER = 5
SLOTS = 4
LANES = 128
FACE_ROWS = QUANTITIES * FACE_PAD
SEND_ROWS = 80
PACK = 32
GROUPS = LANES // PACK
PACKS = 3

OFFSETS = (1, -1, 2, -2)
SEND_ORDER = (2, 1, 3, 0)
F32 = jnp.float32
BF16 = jnp.bfloat16
VMEM = pl.BlockSpec(memory_space=pltpu.VMEM)
NAMES = ("sent_a", "sent_x", "sent_y", "sent_z")


def exchange(sends):
    devices = lax.axis_size("dom")
    receives = {}
    for partner in SEND_ORDER:
        by = OFFSETS[partner]
        pairs = [(i, (i + (by if i % 2 == 0 else -by)) % devices) for i in range(devices)]
        receives[RECEIVED[partner]] = lax.ppermute(sends[NAMES[partner]], "dom", pairs)
    return receives


def split(x):
    high = x.astype(BF16).astype(F32)
    return high, x - high


def wide_basis(matrix):
    high, low = split(matrix)
    return high + pltpu.roll(high, 40, 1) + pltpu.roll(low, 80, 1)


def tall_basis(x):
    high, low = split(x)
    rest = jnp.zeros((LANES - 3 * BASIS_PAD, x.shape[1]), F32)
    return jnp.concatenate([high, low, high, rest], axis=0).astype(BF16)


def wide_faces(matrix):
    high, low = split(matrix)
    return jnp.concatenate([high + pltpu.roll(high, 64, 1), low], axis=1)


def tall_faces(x):
    high, low = split(x)
    return jnp.concatenate([high, low, high], axis=0).astype(BF16)


def matmul(left, right):
    return jnp.dot(left.astype(BF16), right, preferred_element_type=F32)


def matmul_each(left, pieces, group=3):
    left = left.astype(BF16)
    results = []
    for first in range(0, len(pieces), group):
        part = pieces[first : first + group]
        product = matmul(left, side_by_side(part) if len(part) > 1 else part[0])
        results += [product[:, lanes_of(i)] for i in range(len(part))]
    return results


def side_by_side(pieces):
    return jnp.concatenate(pieces, axis=1)


def lanes_of(q):
    return slice(q * LANES, (q + 1) * LANES)


def star_tile(star, work, quantities, groups):
    total = [None] * len(quantities)
    for p in range(groups):
        for d in range(3):
            piece = work[d * BASIS_PAD : (d + 1) * BASIS_PAD, lanes_of(p)]
            for i, q in enumerate(quantities):
                term = star[q, p, d : d + 1, :] * piece
                total[i] = term if total[i] is None else total[i] + term
    return total


def apply_star(star, work, put):
    for first in range(0, QUANTITIES, 3):
        for i, value in enumerate(star_tile(star, work, range(first, first + 3), QUANTITIES)):
            put(first + i, value)


def apply_flux(flux, faces, lift_in):
    for f in range(FACES):
        total = [None] * QUANTITIES
        for p in range(QUANTITIES):
            piece = faces(f, p)
            for q in range(QUANTITIES):
                term = flux[q, p, f : f + 1, :] * piece
                total[q] = term if total[q] is None else total[q] + term
        for q in range(QUANTITIES):
            lift_in[f * FACE_PAD : (f + 1) * FACE_PAD, lanes_of(q)] = total[q]


def lift(lift_w, lift_in):
    return matmul_each(lift_w[0:48, :192], [tall_faces(lift_in[:, lanes_of(q)]) for q in range(QUANTITIES)])


def predict(taylor, star, deriv_w, works):
    for k in range(ORDER):
        for first in range(0, QUANTITIES, 3):
            if k:
                values = star_tile(star, works[k % 2], range(first, first + 3), QUANTITIES)
                for i in range(3):
                    taylor[k, first + i] = values[i]
            else:
                values = [taylor[0, first + i] for i in range(3)]
            if k < ORDER - 1:
                right = side_by_side([tall_basis(value) for value in values])
                works[(k + 1) % 2][:, first * LANES : (first + 3) * LANES] = matmul(deriv_w[...], right)


def integral(taylor, q, j):
    total = None
    for k in range(ORDER):
        weight = ((j + 1) ** (k + 1) - j ** (k + 1)) / math.factorial(k + 1)
        term = taylor[k, q] * weight
        total = term if total is None else total + term
    return total


def step_integral(taylor, q, span):
    total = None
    power = span
    for k in range(ORDER):
        term = taylor[k, q] * (power * (1.0 / math.factorial(k + 1)))
        total = term if total is None else total + term
        power = power * span
    return total


def rotated_faces(turn_w, orientation, integrals, put):
    result = matmul_each(turn_w[...], [tall_basis(value) for value in integrals])
    for q in range(QUANTITIES):
        for g in range(FACES):
            turn = orientation[g : g + 1, :]
            parts = []
            for o in range(3):
                first = (o * FACES + g) * FACE_PAD
                parts.append(result[q][first : first + FACE_PAD, :])
            put(g, q, jnp.where(turn == 0, parts[0], jnp.where(turn == 1, parts[1], parts[2])))


def rows_of(q):
    return slice(q * FACE_PAD, (q + 1) * FACE_PAD)


def take_lanes(source, index):
    if source.shape[0] == 1:
        return take_lanes(jnp.broadcast_to(source, (8, LANES)), index)[0:1, :]
    return jnp.take_along_axis(source, jnp.broadcast_to(index, source.shape), axis=1)


def turn_lanes(x, shift):
    return pltpu.roll(x, shift % LANES, 1) if shift % LANES else x


def choose(pieces, lane, width):
    total = pieces[0]
    for j in range(1, len(pieces)):
        total = jnp.where(lane // width == j, pieces[j], total)
    return total


def pack_sends(faces, index, sends):
    tiles = []
    for row in (0, 2):
        lane = index[row : row + 1, :]
        face = index[row + 1 : row + 2, :]
        tile = take_lanes(faces[0], lane)
        for g in range(1, FACES):
            tile = jnp.where(face == g, take_lanes(faces[g], lane), tile)
        tiles.append(tile)
    lane = lax.broadcasted_iota(jnp.int32, (FACE_PAD, LANES), 1)
    nothing = jnp.zeros((FACE_PAD, LANES), F32)

    def piece(tile, q):
        return tiles[tile][rows_of(q), :] if q < QUANTITIES else nothing

    for k in range(5):
        low, high = piece(0, 2 * k), piece(0, 2 * k + 1)
        sends[0][rows_of(k), :] = choose([low, turn_lanes(high, 64)], lane, 64)
        sends[1][rows_of(k), :] = choose([turn_lanes(low, 64), high], lane, 64)
    for k in range(5):
        for side in range(2):
            value = nothing
            if k < PACKS:
                parts = [turn_lanes(piece(1, 4 * k + j), 32 * j - 64 * side) for j in range(4)]
                value = choose(parts, lane, 32)
            sends[2 + side][rows_of(k), :] = value


def unpack_receives(receives, near, far):
    lane = lax.broadcasted_iota(jnp.int32, (FACE_PAD, LANES), 1)
    for q in range(QUANTITIES):
        ahead, behind = receives[0][rows_of(q // 2), :], receives[1][rows_of(q // 2), :]
        shift = 64 * (q % 2)
        near[rows_of(q), :] = choose([turn_lanes(ahead, shift), turn_lanes(behind, 64 + shift)], lane, 64)
        ahead, behind = receives[2][rows_of(q // 4), :], receives[3][rows_of(q // 4), :]
        shift = -32 * (q % 4)
        far[rows_of(q), :] = choose([turn_lanes(ahead, shift), turn_lanes(behind, 64 + shift)], lane, 64)


def add_remote(index, near, far, collected, put):
    for f in range(FACES):
        place = index[f : f + 1, :]
        lane = jnp.bitwise_and(place, LANES - 1)
        from_near = take_lanes(near[...], lane)
        from_far = take_lanes(far[...], lane)
        remote = jnp.where(place >= LANES, from_far, jnp.where(place >= 0, from_near, 0.0))
        put(f, collected[f] + remote)


def transposed(rows, flip):
    flip[...] = jnp.zeros((LANES, LANES), F32)
    for f in range(FACES):
        flip[f : f + 1, :] = rows[f]
    return flip[...].T


def ranks(keys, flip):
    columns = transposed(keys, flip)
    result = []
    for f in range(FACES):
        total = None
        for other in range(FACES):
            less = jnp.where(columns[:, other : other + 1] < keys[f], 1.0, 0.0)
            total = less if total is None else total + less
        result.append(jnp.sum(total, axis=0, keepdims=True))
    return result


def group_places(groups, keys, flip):
    bases = (0.0, 64.0, 128.0, 192.0)
    order = ranks([groups[f] * 512.0 + keys[f] for f in range(FACES)], flip)
    sizes = []
    for partner in range(FACES):
        total = None
        for f in range(FACES):
            here = jnp.where(groups[f] == partner, 1.0, 0.0)
            total = here if total is None else total + here
        sizes.append(jnp.sum(total, axis=1, keepdims=True))
    places = []
    for f in range(FACES):
        place = jnp.full((1, LANES), -1.0, F32)
        start = jnp.zeros((1, 1), F32)
        for partner in range(FACES):
            place = jnp.where(groups[f] == partner, order[f] - start + bases[partner], place)
            start = start + sizes[partner]
        places.append(place)
    return places


def partner_groups(devices, neighbour, face_kind):
    here = lax.axis_index("dom")
    sign = 1 - 2 * jnp.bitwise_and(here, 1)
    targets = [jnp.where(sign * by < 0, sign * by + devices, sign * by) for by in OFFSETS]
    sources = targets[:2] + [devices - far for far in targets[2:]]
    send_groups, recv_groups, local = [], [], []
    for f in range(FACES):
        interior = face_kind[f : f + 1, :] == 0
        distance = lax.shift_right_logical(neighbour[f : f + 1, :], 7) - here
        distance = jnp.where(distance < 0, distance + devices, distance)
        send = jnp.full((1, LANES), 4, jnp.int32)
        recv = jnp.full((1, LANES), 4, jnp.int32)
        for partner in range(4):
            send = jnp.where(interior & (distance == targets[partner]), partner, send)
            recv = jnp.where(interior & (distance == sources[partner]), partner, recv)
        send_groups.append(send.astype(F32))
        recv_groups.append(recv.astype(F32))
        local.append(interior & (distance == 0))
    return send_groups, recv_groups, local


def make_send_index(devices, neighbour, face_kind, index, flip, spare):
    groups, _, _ = partner_groups(devices, neighbour, face_kind)
    element = lax.broadcasted_iota(jnp.int32, (1, LANES), 1)
    keys = [(element + f * LANES).astype(F32) for f in range(FACES)]
    places = group_places(groups, keys, flip)
    for tile, (element, face) in enumerate(columns_of(places, spare)):
        index[2 * tile : 2 * tile + 1, :] = element
        index[2 * tile + 1 : 2 * tile + 2, :] = face


def columns_of(places, flip):
    columns = transposed(places, flip)
    row = lax.broadcasted_iota(jnp.int32, (LANES, LANES), 0).astype(F32)
    lane = lax.broadcasted_iota(jnp.int32, (LANES, LANES), 1).astype(F32)
    result = []
    for tile in range(2):
        total = None
        for f in range(FACES):
            hit = jnp.where(columns[:, f : f + 1] == lane + tile * 128.0, row + f * 128.0, 0.0)
            total = hit if total is None else total + hit
        code = jnp.sum(total, axis=0, keepdims=True).astype(jnp.int32)
        result.append((jnp.bitwise_and(code, LANES - 1), lax.shift_right_logical(code, 7)))
    return result


def make_recv_index(devices, neighbour, neighbour_face, face_kind, index, flip):
    _, groups, local = partner_groups(devices, neighbour, face_kind)
    index[...] = jnp.zeros((24, LANES), jnp.int32)
    keys = []
    for f in range(FACES):
        far_face = neighbour_face[f : f + 1, :]
        far_element = jnp.bitwise_and(neighbour[f : f + 1, :], LANES - 1)
        keys.append((far_face * LANES + far_element).astype(F32))
        index[8 + f : 9 + f, :] = far_element
        index[16 + f : 17 + f, :] = jnp.where(local[f], far_face, -1)
    places = group_places(groups, keys, flip)
    for f in range(FACES):
        index[f : f + 1, :] = places[f].astype(jnp.int32)


def make_deriv(deriv, frame, deriv_w):
    deriv_w[...] = frame[...]
    for d in range(3):
        deriv_w[d * BASIS_PAD : d * BASIS_PAD + BASIS, :BASIS] = -deriv[d]
    deriv_w[...] = wide_basis(deriv_w[...])


def make_faces(proj, orient, frame, proj_w, turn_w, flip):
    proj_w[...] = frame[0:64, :]
    for g in range(FACES):
        proj_w[g * FACE_PAD : g * FACE_PAD + FACE_BASIS, :BASIS] = proj[:, g, :]
    right = side_by_side([proj_w[rows_of(g), :] for g in range(FACES)])
    flip[...] = frame[...]
    for o in range(3):
        flip[o * FACE_PAD : o * FACE_PAD + FACE_BASIS, :FACE_BASIS] = orient[o]
    turned = jnp.dot(
        flip[0:48, :FACE_PAD], right, precision=lax.Precision.HIGHEST, preferred_element_type=F32
    )
    for o in range(3):
        for g in range(FACES):
            turn_w[rows_of(o * FACES + g), :] = wide_basis(turned[rows_of(o), lanes_of(g)])
    proj_w[...] = wide_basis(proj_w[...])


def make_update(update, update_w, flips):
    update_w[...] = jnp.zeros((LANES, LANES), F32)
    for d in range(3):
        flip = flips.at[d]
        flip[...] = jnp.zeros((LANES, LANES), F32)
        flip[:BASIS, :BASIS] = update[d]
        update_w[d * BASIS_PAD : (d + 1) * BASIS_PAD, :] = flip[...].T[:BASIS_PAD, :]
    update_w[...] = wide_basis(update_w[...])


def make_lift(lift_mat, deriv_w, lift_w, flips):
    total = None
    for f in range(FACES):
        flip = flips.at[f]
        flip[...] = jnp.zeros((LANES, LANES), F32)
        flip[:FACE_BASIS, :BASIS] = lift_mat[:, f, :]
        value = turn_lanes(flip[...].T[0:48, :], 16 * f)
        total = value if total is None else total + value
    lift_w[0:48, :] = wide_faces(total)
    lift_w[48:176, :] = wide_faces(matmul(deriv_w[...], tall_basis(total[0:BASIS_PAD, :])))


def pack(pieces, element, lane):
    return choose([take_lanes(piece, element) for piece in pieces], lane, PACK)


def pack_quantities(pieces, element):
    lane = lax.broadcasted_iota(jnp.int32, pieces[0].shape, 1)
    nothing = jnp.zeros(pieces[0].shape, F32)
    result = []
    for k in range(PACKS):
        group = [take_lanes(pieces[q], element) if q < QUANTITIES else nothing for q in range(4 * k, 4 * k + 4)]
        result.append(choose(group, lane, PACK))
    return result


def unpack_quantity(packed, q, rank):
    return take_lanes(packed(q // 4), rank + PACK * (q % 4))


def make_packs(r):
    row = lax.broadcasted_iota(jnp.int32, (LANES, LANES), 0).astype(F32)
    lane = lax.broadcasted_iota(jnp.int32, (LANES, LANES), 1)
    cluster = r.cluster[...].astype(F32)
    columns = transposed([cluster] * FACES, r.flips.at[8])
    before = jnp.where((columns[:, 0:1] == cluster) & (row < lane.astype(F32)), 1.0, 0.0)
    rank = jnp.sum(before, axis=0, keepdims=True)
    columns = transposed([cluster * 64.0 + rank] * FACES, r.flips.at[9])
    r.packs[...] = jnp.zeros((8, LANES), jnp.int32)
    for block in range(2):
        wanted = jnp.bitwise_and(lane, PACK - 1).astype(F32) + 64.0 * block
        hit = jnp.where(columns[:, 0:1] == wanted, row, 0.0)
        r.packs[block : block + 1, :] = jnp.sum(hit, axis=0, keepdims=True).astype(jnp.int32)
    rank = rank.astype(jnp.int32)
    r.packs[2:3, :] = jnp.bitwise_and(rank, PACK - 1)
    lane = lax.broadcasted_iota(jnp.int32, (1, LANES), 1)
    kinds = r.cluster[...]
    for f in range(FACES):
        r.source_cluster[f : f + 1, :] = take_lanes(kinds, r.index[8 + f : 9 + f, :])
    got = [r.index[f : f + 1, :].astype(F32) for f in range(FACES)]
    for tile, (element, _) in enumerate(columns_of(got, r.flips.at[10])):
        kind = take_lanes(kinds, element)
        for side in range(2):
            width = 32 if tile else 64
            parts = [turn_lanes(kind, width * j - 64 * side) for j in range(LANES // width)]
            first = 2 * tile + side
            r.column_cluster[first : first + 1, :] = choose(parts, lane, width)
    for tile in range(2):
        element = r.send_index[2 * tile : 2 * tile + 1, :]
        face = r.send_index[2 * tile + 1 : 2 * tile + 2, :]
        kind = take_lanes(kinds, element)
        order = take_lanes(jnp.bitwise_and(rank, PACK - 1), element)
        rows = [order] + [jnp.where(kind == block, face, -1) for block in range(2)]
        for side in range(2):
            width = 32 if tile else 64
            for i in range(3):
                parts = [turn_lanes(rows[i], width * j - 64 * side) for j in range(LANES // width)]
                value = choose(parts, lane, width)
                if i == 0:
                    value = value + PACK * (lane // width)
                first = 3 * (2 * tile + side) + i
                r.send_packs[first : first + 1, :] = value


def pack_flux(flux, element, packed):
    lane = lax.broadcasted_iota(jnp.int32, (FACES, LANES), 1)
    face = lax.broadcasted_iota(jnp.int32, (FACES, LANES), 0)
    for q in range(QUANTITIES):
        for p in range(QUANTITIES):
            value = jnp.where(face == lane // PACK, take_lanes(flux[q, p], element), 0.0)
            packed[q, p : p + 1, :] = jnp.sum(value, axis=0, keepdims=True)


def pack_block(r, block, where, star, flux):
    element = r.packs[block : block + 1, :]
    lane = lax.broadcasted_iota(jnp.int32, (1, LANES), 1)
    where[...] = jnp.zeros((8, LANES), jnp.int32)
    where[0:1, :] = pack([r.index[f : f + 1, :] for f in range(FACES)], element, lane)
    where[1:5, :] = take_lanes(r.orientation[...], element)
    where[5:6, :] = pack([r.index[8 + f : 9 + f, :] for f in range(FACES)], element, lane)
    where[6:7, :] = pack([r.index[16 + f : 17 + f, :] for f in range(FACES)], element, lane)
    for q in range(QUANTITIES):
        for k, value in enumerate(pack_quantities([r.star[q, p] for p in range(QUANTITIES)], element)):
            star[q, k] = value
    pack_flux(r.flux_neigh, element, flux)


def spread_faces(total, lift_in):
    lane = lax.broadcasted_iota(jnp.int32, (FACE_PAD, LANES), 1)
    nothing = jnp.zeros((FACE_PAD, LANES), F32)
    for k in range(PACKS):
        for f in range(FACES):
            parts = []
            for j in range(GROUPS):
                q = GROUPS * k + j
                parts.append(turn_lanes(total[q], PACK * (j - f)) if q < QUANTITIES else nothing)
            lift_in[f * FACE_PAD : (f + 1) * FACE_PAD, lanes_of(k)] = choose(parts, lane, PACK)
    return [tall_faces(lift_in[:, lanes_of(k)]) for k in range(PACKS)]


def packed_fields(r, block, base, ahead, gathered, flux, where, lift_in, work):
    near_refs = (r.got_a, r.got_x) if block == 0 else (r.sum_a, r.sum_x)
    far_refs = (r.got_y, r.got_z) if block == 0 else (r.sum_y, r.sum_z)
    place = where[0:1, :]
    near = jnp.bitwise_and(place, 63)
    far = jnp.bitwise_and(place, PACK - 1)
    total = [None] * QUANTITIES
    for p in range(QUANTITIES):
        got = [take_lanes(ref[rows_of(p // 2), :], near + 64 * (p % 2)) for ref in near_refs]
        got += [take_lanes(ref[rows_of(p // 4), :], far + PACK * (p % 4)) for ref in far_refs]
        remote = jnp.where(place < 64, got[0], jnp.where(place < 128, got[1], jnp.where(place < 192, got[2], got[3])))
        piece = gathered[rows_of(p), :] + jnp.where(place >= 0, remote, 0.0)
        for q in range(QUANTITIES):
            term = flux[q, p : p + 1, :] * piece
            total[q] = term if total[q] is None else total[q] + term
    lifted = matmul_each(r.lift_w[:, :192], spread_faces(total, lift_in), 1)
    for k in range(PACKS):
        work[:, lanes_of(k)] = ahead[:, lanes_of(k)] - lifted[k][48:176, :]
    return [base[k] - lifted[k][:BASIS_PAD, :] for k in range(PACKS)]


def packed_derivatives(terms, deriv_w, work):
    for k in range(PACKS):
        work[:, lanes_of(k)] = matmul(deriv_w[...], tall_basis(terms[k]))


def gather_copies(values):
    lane = lax.broadcasted_iota(jnp.int32, (BASIS_PAD, LANES), 1)
    if len(values) == 1:
        value = values[0]
        rolled = [pltpu.roll(value, PACK * shift, 1) for shift in (1, 2, 3)]
        return jnp.where(lane < PACK, (value + rolled[0]) + (rolled[1] + rolled[2]), 0.0)
    parts = []
    for shift in range(GROUPS):
        mixed = choose([values[(copy + shift) % GROUPS] for copy in range(GROUPS)], lane, PACK)
        parts.append(turn_lanes(mixed, PACK * shift))
    return (parts[0] + parts[1]) + (parts[2] + parts[3])


def packed_star(star, work, follow=None):
    result = []
    for k in range(PACKS):
        quantities = range(GROUPS * k, min(GROUPS * (k + 1), QUANTITIES))
        result.append(gather_copies(star_tile(star, work, quantities, PACKS)))
        if follow is not None:
            follow(k, result[k])
    return result


def packed_faces(integrals, turn_w, where, put):
    result = matmul_each(turn_w[...], [tall_basis(value) for value in integrals], 1)
    for k in range(PACKS):
        for g in range(FACES):
            turn = where[1 + g : 2 + g, :]
            parts = [result[k][rows_of(o * FACES + g), :] for o in range(3)]
            put(g, k, jnp.where(turn == 0, parts[0], jnp.where(turn == 1, parts[1], parts[2])))


def add_terms(total, terms, weight):
    values = [term * weight for term in terms]
    return values if total is None else [a + b for a, b in zip(total, values)]


def add_received(r):
    for name in "axyz":
        getattr(r, "sum_" + name)[...] = getattr(r, "got_" + name)[...] + getattr(r, "old_" + name)[...]


def slot_kernel(slot, r):
    if slot == 2:
        add_received(r)
    numbers = (0, 1) if slot == 2 else (0,)
    names = ("base", "ahead", "gathered", "flux", "where", "lift_in", "star", "fields", "step", "faces", "work", "spare")
    blocks = [types.SimpleNamespace(**{name: getattr(r, name + str(b)) for name in names}) for b in numbers]
    terms = []
    for b, block in enumerate(blocks):
        terms.append(
            packed_fields(
                r, b, block.base, block.ahead, block.gathered, block.flux, block.where, block.lift_in, block.work
            )
        )
        for k in range(PACKS):
            block.fields[k] = terms[-1][k]
    first = [None] * len(blocks)
    second = None
    for k in range(ORDER):
        for b, block in enumerate(blocks):
            if k:
                work, other = (block.work, block.spare) if k % 2 else (block.spare, block.work)

                def follow(i, value, other=other):
                    other[:, lanes_of(i)] = matmul(r.deriv_w[...], tall_basis(value))

                terms[b] = packed_star(block.star, work, follow if k < ORDER - 1 else None)
            first[b] = add_terms(first[b], terms[b], 1.0 / math.factorial(k + 1))
        if slot == 2:
            second = add_terms(second, terms[1], (2.0 ** (k + 1) - 1.0) / math.factorial(k + 1))
    for b, block in enumerate(blocks):

        def put(g, k, value, faces=block.faces):
            faces[g, rows_of(k), :] = value

        packed_faces(first[b], r.turn_w, block.where, put)
        for k in range(PACKS):
            block.step[k] = first[b][k]
    if slot == 2:
        for k in range(PACKS):
            r.second1[k] = second[k]
    for partner in SEND_ORDER:
        later, sent = getattr(r, "later_" + NAMES[partner]), getattr(r, NAMES[partner])
        near = partner < 2
        lane = r.send_packs[3 * partner : 3 * partner + 1, :]
        for k in range(5 if near else PACKS):
            value = later[rows_of(k), :]
            source = k // 2 if near else k
            place = lane + 64 * (k % 2) if near else lane
            for b, block in enumerate(blocks):
                face = r.send_packs[3 * partner + 1 + b : 3 * partner + 2 + b, :]
                for g in range(FACES):
                    value = jnp.where(face == g, take_lanes(block.faces[g, rows_of(source), :], place), value)
            sent[rows_of(k), :] = value
        if not near:
            sent[48:80, :] = jnp.zeros((32, LANES), F32)


def frame_kernel(r):
    r.frame[...] = jnp.zeros((LANES, LANES), F32)


def first_kernel(devices, r):
    make_deriv(r.deriv, r.frame, r.deriv_w)
    for q in range(QUANTITIES):
        r.taylor[0, q] = jnp.zeros((BASIS_PAD, LANES), F32)
        r.taylor[0, q, :BASIS, :] = r.dofs[q]
    r.orientation_out[...] = r.orientation[...]
    r.cluster_out[...] = r.cluster[...].reshape(1, LANES)
    r.far_out[...] = r.neighbour_face[...]
    make_send_index(devices, r.neighbour, r.face_kind, r.send_index, r.flip, r.flap)
    make_faces(r.proj, r.orient, r.frame, r.proj_w, r.turn_w, r.flop)
    predict(r.taylor, r.star, r.deriv_w, (r.spare, r.work))
    span = lax.shift_left(jnp.ones_like(r.cluster_out[...]), r.cluster_out[...]).astype(F32)
    for q in range(QUANTITIES):
        r.step[q] = step_integral(r.taylor, q, span)

    def put(g, q, value):
        r.faces[g, rows_of(q), :] = value

    rotated_faces(r.turn_w, r.orientation, [integral(r.taylor, q, 0) for q in range(QUANTITIES)], put)
    pack_sends(r.faces, r.send_index, [getattr(r, name) for name in NAMES])


def last_kernel(r):
    add_received(r)
    unpack_receives([r.sum_a, r.sum_x, r.sum_y, r.sum_z], r.near, r.far)

    def keep(f, value):
        r.collected[f] = value

    add_remote(r.index, r.near, r.far, r.gathered, keep)
    apply_flux(r.flux_neigh, lambda f, p: r.collected[f, rows_of(p), :], r.lift_in)
    lifted = lift(r.lift_w, r.lift_in)
    for q in range(QUANTITIES):
        r.out[q] = (r.base[q] - lifted[q][:BASIS_PAD, :])[:BASIS, :]


def later_faces(r, j, later):
    def store(g, q, value):
        later[g, rows_of(q), :] = value

    rotated_faces(r.turn_w, r.orientation, [integral(r.taylor, q, j) for q in range(QUANTITIES)], store)


def beside_kernel(slot, devices, r):
    if slot == 0:
        make_update(r.update, r.update_w, r.flips.at[0:3])
        make_lift(r.lift_mat, r.deriv_w, r.lift_w, r.flips.at[3:7])
        make_recv_index(devices, r.neighbour, r.neighbour_face, r.face_kind, r.index, r.flips.at[7])
        make_packs(r)
        pack_block(r, 0, r.where0, r.star0, r.flux0)
        mirror = jnp.where(r.face_kind[...] == 1, 1.0, 0.0)
        for p in range(QUANTITIES):
            sign = -mirror if p < 6 else mirror
            for q in range(QUANTITIES):
                r.flux_own[q, p] = r.flux_local[q, p] + sign * r.flux_neigh[q, p]
    cluster = r.cluster[...]
    started = cluster <= (0 if slot % 2 else 1)
    rank = r.packs[2:3, :]

    def unpacked(name, q, rows=None):
        def packed(ref):
            return (lambda k: ref[k]) if rows is None else (lambda k: ref[rows, rows_of(k), :])

        value = unpack_quantity(packed(getattr(r, name + "0")), q, rank)
        if slot == 2:
            value = jnp.where(cluster == 1, unpack_quantity(packed(getattr(r, name + "1")), q, rank), value)
        return value

    sums = r.sums
    for g in range(FACES):
        reset = r.source_cluster[g : g + 1, :] <= (0 if slot % 2 else 1)
        for q in range(QUANTITIES):
            if slot == 0:
                sums[g, rows_of(q), :] = r.faces[g, rows_of(q), :]
                continue
            value = jnp.where(started, unpacked("faces", q, g), r.later[g, rows_of(q), :])
            sums[g, rows_of(q), :] = value + jnp.where(reset, 0.0, r.old_sums[g, rows_of(q), :])
    if slot:
        for i, name in enumerate("axyz"):
            reset = r.column_cluster[i : i + 1, :] <= (0 if slot % 2 else 1)
            total = getattr(r, "sum_" + name)[...] if slot == 2 else getattr(r, "got_" + name)[...]
            if slot == 3:
                total = total + getattr(r, "older_" + name)[...]
            getattr(r, "old_" + name)[...] = jnp.where(reset, 0.0, total)
    if slot == 3:
        for f in range(FACES):
            lane = r.index[8 + f : 9 + f, :]
            face = r.index[16 + f : 17 + f, :]
            total = None
            for g in range(FACES):
                value = jnp.where(face == g, take_lanes(sums[g], lane), 0.0)
                total = value if total is None else total + value
            r.gathered[f] = total
    if slot == 0:
        fields = [r.taylor[0, q] for q in range(QUANTITIES)]
        steps = [r.step[q] for q in range(QUANTITIES)]
    else:
        fields = [unpacked("fields", q) for q in range(QUANTITIES)]
        steps = [unpacked("step", q) for q in range(QUANTITIES)]
        if slot == 2:
            for q in range(QUANTITIES):
                steps[q] = steps[q] + jnp.where(cluster == 1, unpack_quantity(lambda k: r.second1[k], q, rank), 0.0)
    right = [tall_basis(value) for value in steps]
    own = matmul_each(r.proj_w[...], right)
    apply_flux(r.flux_own, lambda f, p: own[p][rows_of(f), :], r.lift_in)
    lifted = lift(r.lift_w, r.lift_in)
    for q, value in enumerate(matmul_each(r.update_w[...], right)):
        r.work[:, lanes_of(q)] = value

    def put(q, value):
        value = fields[q] + value - lifted[q][:BASIS_PAD, :]
        r.base[q] = value if slot == 0 else jnp.where(started, value, r.old_base[q])

    apply_star(r.star, r.work, put)
    if slot == 1:
        pack_block(r, 1, r.where1, r.star1, r.flux1)
    if slot == 0:
        later_faces(r, 1, r.later1)
    if slot == 1:
        later_faces(r, 2, r.later2)
        later_faces(r, 3, r.later3)
    if slot == 2:

        def merge(g, q, value):
            r.next_later[g, rows_of(q), :] = jnp.where(cluster == 1, value, r.after[g, rows_of(q), :])

        rotated_faces(
            r.turn_w,
            r.orientation,
            [unpack_quantity(lambda k: r.second1[k], q, rank) for q in range(QUANTITIES)],
            merge,
        )
    if slot == 3:
        return
    later = r.later1 if slot == 0 else r.later2 if slot == 1 else r.next_later
    pack_sends(later, r.send_index, [getattr(r, "later_" + name) for name in NAMES])
    targets = [(r.base0, r.ahead0, r.gathered0, r.where0)]
    if slot == 1:
        targets.append((r.base1, r.ahead1, r.gathered1, r.where1))
    for block, (base, ahead, gathered, where) in enumerate(targets):
        packed = pack_quantities([r.base[q] for q in range(QUANTITIES)], r.packs[block : block + 1, :])
        for k in range(PACKS):
            base[k] = packed[k]
        packed_derivatives(packed, r.deriv_w, ahead)
        lane, face = where[5:6, :], where[6:7, :]
        total = None
        for g in range(FACES):
            value = jnp.where(face == g, take_lanes(sums[g], lane), 0.0)
            total = value if total is None else total + value
        gathered[...] = total


def shape_of(array):
    return jax.ShapeDtypeStruct(array.shape, array.dtype)


def shape(*dims):
    return jax.ShapeDtypeStruct(dims, F32)


def ints(rows):
    return jax.ShapeDtypeStruct((rows, LANES), jnp.int32)


RECEIVED = ("got_a", "got_x", "got_y", "got_z")
TAYLOR = shape(ORDER, QUANTITIES, BASIS_PAD, LANES)
STATE = shape(QUANTITIES, BASIS_PAD, LANES)
PACKED = shape(PACKS, BASIS_PAD, LANES)
AHEAD = shape(LANES, PACKS * LANES)
PACKED_STAR = shape(QUANTITIES, PACKS, 3, LANES)
PACKED_FLUX = shape(QUANTITIES, QUANTITIES, LANES)
PACKED_LIFT = shape(FACES * FACE_PAD, PACKS * LANES)
TURNED = shape(FACES, FACE_ROWS, LANES)
TILE = shape(FACE_ROWS, LANES)
SQUARE = shape(LANES, LANES)
WORK = shape(LANES, QUANTITIES * LANES)
LIFT_IN = shape(FACES * FACE_PAD, QUANTITIES * LANES)
SENDS = {NAMES[i]: shape(SEND_ROWS, LANES) for i in SEND_ORDER}
OLD = {"old_" + name: shape(SEND_ROWS, LANES) for name in "axyz"}
SUMS = {"sum_" + name: shape(SEND_ROWS, LANES) for name in "axyz"}
LATER_SENDS = {"later_" + name: value for name, value in SENDS.items()}
EARLY_FLOPS = 5_000_000_000


def call(kernel, name, ins, outs, scratch, flops):
    names = [*ins, *outs, *scratch]
    size = sum(math.prod(a.shape) * 4 for a in [*ins.values(), *outs.values()])

    def run(*refs):
        kernel(types.SimpleNamespace(**dict(zip(names, refs))))

    result = pl.pallas_call(
        run,
        out_shape=list(outs.values()),
        in_specs=[VMEM] * len(ins),
        out_specs=[VMEM] * len(outs),
        scratch_shapes=[pltpu.VMEM(a.shape, a.dtype) for a in scratch.values()],
        compiler_params=pltpu.CompilerParams(vmem_limit_bytes=32 * 1024 * 1024),
        cost_estimate=pl.CostEstimate(flops=flops, bytes_accessed=size, transcendentals=0),
        name=name,
    )(*ins.values())
    return dict(zip(outs, result))


def some(values, *names):
    return {name: values[name] for name in names}


def body(
    dofs, star, flux_local, flux_neigh, neighbour, neighbour_face, orientation, face_kind, cluster,
    deriv_stiff, update_stiff, face_proj, face_lift, orient_map,
):
    devices = lax.axis_size("dom")
    star, flux_local, flux_neigh = [jnp.transpose(a, (1, 2, 0, 3)) for a in (star, flux_local, flux_neigh)]
    face_proj, face_lift = jnp.transpose(face_proj, (1, 0, 2)), jnp.transpose(face_lift, (2, 0, 1))
    v = dict(
        star=star, flux_local=flux_local, flux_neigh=flux_neigh, neighbour=neighbour,
        face_kind=face_kind, update=update_stiff, lift_mat=face_lift,
    )
    frame = call(frame_kernel, "frame", {}, dict(frame=SQUARE), {}, EARLY_FLOPS)["frame"]
    sends = call(
        functools.partial(first_kernel, devices),
        "start",
        dict(frame=frame, neighbour=neighbour, neighbour_face=neighbour_face, face_kind=face_kind,
             orientation=orientation, cluster=cluster, deriv=deriv_stiff, proj=face_proj, orient=orient_map,
             dofs=dofs, star=star),
        dict(deriv_w=SQUARE, far_out=ints(FACES), proj_w=shape(64, LANES), turn_w=shape(192, LANES),
             send_index=ints(8), orientation_out=ints(FACES), cluster_out=ints(1),
             taylor=TAYLOR, step=STATE, faces=TURNED, **SENDS),
        dict(work=WORK, spare=WORK, flip=SQUARE, flap=SQUARE, flop=SQUARE),
        100_000_000,
    )
    v.update(some(sends, "deriv_w", "proj_w", "turn_w", "send_index"), orientation=sends["orientation_out"],
             cluster=sends["cluster_out"], neighbour_face=sends["far_out"])
    receives = exchange(sends)
    kept = call(
        functools.partial(beside_kernel, 0, devices),
        "beside0",
        {**some(sends, "taylor", "step", "faces"),
         **some(v, "star", "orientation", "cluster", "flux_local", "flux_neigh", "face_kind", "neighbour",
                "neighbour_face", "update", "lift_mat", "deriv_w", "proj_w", "turn_w", "send_index")},
        dict(base=STATE, sums=TURNED, source_cluster=ints(FACES), column_cluster=ints(4),
             flux_own=shape_of(flux_local), later1=TURNED, update_w=SQUARE, lift_w=shape(176, 256), index=ints(24), packs=ints(8),
             send_packs=ints(12), where0=ints(8), star0=PACKED_STAR, flux0=PACKED_FLUX,
             base0=PACKED, ahead0=AHEAD, gathered0=TILE, **LATER_SENDS),
        dict(work=WORK, lift_in=LIFT_IN, flips=shape(11, LANES, LANES)),
        50_000_000,
    )
    v.update(kept)
    v.update(taylor=sends["taylor"])
    for slot in range(1, SLOTS):
        numbers = (0, 1) if slot == 2 else (0,)
        per_block = [name + str(b) for b in numbers for name in ("base", "ahead", "gathered", "flux", "star", "where")]
        outs, scratch = {}, {}
        for b in numbers:
            outs.update({"fields%d" % b: PACKED, "step%d" % b: PACKED, "faces%d" % b: shape(FACES, 48, LANES)})
            scratch.update(
                {"work%d" % b: AHEAD, "spare%d" % b: AHEAD, "lift_in%d" % b: PACKED_LIFT}
            )
        if slot == 2:
            outs["second1"] = PACKED
        sends = call(
            functools.partial(slot_kernel, slot),
            "slot%d" % slot,
            {**receives, **(some(v, *OLD) if slot == 2 else {}),
             **some(v, *per_block, *LATER_SENDS, "deriv_w", "turn_w", "lift_w", "send_packs")},
            {**outs, **(SUMS if slot == 2 else {}), **SENDS},
            scratch,
            100_000_000,
        )
        previous, receives = receives, exchange(sends)
        ins = some(sends, *outs, *(SUMS if slot == 2 else ()))
        if slot != 2:
            ins.update(previous)
        if slot == 3:
            ins.update({"older_" + name: v["old_" + name] for name in "axyz"})
        ins.update(old_base=v["base"], old_sums=v["sums"], later=v["later%d" % slot])
        ins.update(
            some(v, "star", "cluster", "flux_own", "proj_w", "update_w", "lift_w", "packs", "source_cluster",
                 "column_cluster")
        )
        results = dict(base=STATE, **OLD)
        scratch = dict(work=WORK, lift_in=LIFT_IN)
        if slot < 3:
            ins.update(some(v, "send_index", "deriv_w", "where0"))
            results.update(sums=TURNED, base0=PACKED, ahead0=AHEAD, gathered0=TILE, **LATER_SENDS)
        else:
            ins.update(some(v, "index"))
            results.update(gathered=TURNED)
            scratch.update(sums=TURNED)
        if slot == 1:
            ins.update(some(v, "flux_neigh", "orientation", "index", "turn_w", "taylor"))
            results.update(later2=TURNED, later3=TURNED, base1=PACKED, ahead1=AHEAD, gathered1=TILE, where1=ints(8), star1=PACKED_STAR,
                           flux1=PACKED_FLUX)
        if slot == 2:
            ins.update(after=v["later3"], **some(v, "orientation", "turn_w"))
            results.update(next_later=TURNED)
        v.update(
            call(
                functools.partial(beside_kernel, slot, devices), "beside%d" % slot, ins, results,
                scratch, 50_000_000,
            )
        )
        if slot == 2:
            v["later3"] = v["next_later"]
    return call(
        last_kernel,
        "finish",
        {**receives, **some(v, *OLD, "base", "gathered", "flux_neigh", "lift_w", "index")},
        dict(out=shape(*dofs.shape)),
        dict(**SUMS, near=TILE, far=TILE, collected=TURNED, lift_in=LIFT_IN),
        10_000_000,
    )["out"]


def solution(mesh):
    in_specs = (
        P(None, None, "dom"),
        P(None, None, None, "dom"),
        P(None, None, None, "dom"),
        P(None, None, None, "dom"),
        P(None, "dom"),
        P(None, "dom"),
        P(None, "dom"),
        P(None, "dom"),
        P("dom"),
        P(),
        P(),
        P(),
        P(),
        P(),
    )
    out_specs = P(None, None, "dom")
    return jax.shard_map(body, mesh=mesh, in_specs=in_specs, out_specs=out_specs, check_vma=False)
```

```python
import functools
import math
import types

import jax
import jax.numpy as jnp
from jax import lax
from jax.experimental import pallas as pl
from jax.experimental.pallas import tpu as pltpu
from jax.sharding import PartitionSpec as P

CAP_NEAR = 64
CAP_FAR = 32
QUANTITIES = 9
BASIS = 35
BASIS_PAD = 40
FACE_BASIS = 15
FACE_PAD = 16
FACES = 4
ORDER = 5
SLOTS = 4
LANES = 128
FACE_ROWS = QUANTITIES * FACE_PAD
SEND_ROWS = 80
PACK = 32
GROUPS = LANES // PACK
PACKS = 3

OFFSETS = (1, -1, 2, -2)
SEND_ORDER = (2, 1, 3, 0)
F32 = jnp.float32
BF16 = jnp.bfloat16
VMEM = pl.BlockSpec(memory_space=pltpu.VMEM)
NAMES = ("sent_a", "sent_x", "sent_y", "sent_z")


def exchange(sends):
    devices = lax.axis_size("dom")
    receives = {}
    for partner in SEND_ORDER:
        by = OFFSETS[partner]
        pairs = [(i, (i + (by if i % 2 == 0 else -by)) % devices) for i in range(devices)]
        receives[RECEIVED[partner]] = lax.ppermute(sends[NAMES[partner]], "dom", pairs)
    return receives


def split(x):
    high = x.astype(BF16).astype(F32)
    return high, x - high


def wide_basis(matrix):
    high, low = split(matrix)
    return high + pltpu.roll(high, 40, 1) + pltpu.roll(low, 80, 1)


def tall_basis(x):
    high, low = split(x)
    rest = jnp.zeros((LANES - 3 * BASIS_PAD, x.shape[1]), F32)
    return jnp.concatenate([high, low, high, rest], axis=0).astype(BF16)


def wide_faces(matrix):
    high, low = split(matrix)
    return jnp.concatenate([high + pltpu.roll(high, 64, 1), low], axis=1)


def tall_faces(x):
    high, low = split(x)
    return jnp.concatenate([high, low, high], axis=0).astype(BF16)


def matmul(left, right):
    return jnp.dot(left.astype(BF16), right, preferred_element_type=F32)


def matmul_each(left, pieces, group=3):
    left = left.astype(BF16)
    results = []
    for first in range(0, len(pieces), group):
        part = pieces[first : first + group]
        product = matmul(left, side_by_side(part) if len(part) > 1 else part[0])
        results += [product[:, lanes_of(i)] for i in range(len(part))]
    return results


def side_by_side(pieces):
    return jnp.concatenate(pieces, axis=1)


def lanes_of(q):
    return slice(q * LANES, (q + 1) * LANES)


def star_tile(star, work, quantities, groups):
    total = [None] * len(quantities)
    for p in range(groups):
        for d in range(3):
            piece = work[d * BASIS_PAD : (d + 1) * BASIS_PAD, lanes_of(p)]
            for i, q in enumerate(quantities):
                term = star[q, p, d : d + 1, :] * piece
                total[i] = term if total[i] is None else total[i] + term
    return total


def apply_star(star, work, put):
    for first in range(0, QUANTITIES, 3):
        for i, value in enumerate(star_tile(star, work, range(first, first + 3), QUANTITIES)):
            put(first + i, value)


def apply_flux(flux, faces, lift_in):
    for f in range(FACES):
        total = [None] * QUANTITIES
        for p in range(QUANTITIES):
            piece = faces(f, p)
            for q in range(QUANTITIES):
                term = flux[q, p, f : f + 1, :] * piece
                total[q] = term if total[q] is None else total[q] + term
        for q in range(QUANTITIES):
            lift_in[f * FACE_PAD : (f + 1) * FACE_PAD, lanes_of(q)] = total[q]


def lift(lift_w, lift_in):
    return matmul_each(lift_w[0:48, :192], [tall_faces(lift_in[:, lanes_of(q)]) for q in range(QUANTITIES)])


def predict(taylor, star, deriv_w, works, between):
    for k in range(ORDER):
        if k in between:
            between[k]()
        for first in range(0, QUANTITIES, 3):
            if k:
                values = star_tile(star, works[k % 2], range(first, first + 3), QUANTITIES)
                for i in range(3):
                    taylor[k, first + i] = values[i]
            else:
                values = [taylor[0, first + i] for i in range(3)]
            if k < ORDER - 1:
                right = side_by_side([tall_basis(value) for value in values])
                works[(k + 1) % 2][:, first * LANES : (first + 3) * LANES] = matmul(deriv_w[...], right)


def integral(taylor, q, j):
    total = None
    for k in range(ORDER):
        weight = ((j + 1) ** (k + 1) - j ** (k + 1)) / math.factorial(k + 1)
        term = taylor[k, q] * weight
        total = term if total is None else total + term
    return total


def step_integral(taylor, q, span):
    total = None
    power = span
    for k in range(ORDER):
        term = taylor[k, q] * (power * (1.0 / math.factorial(k + 1)))
        total = term if total is None else total + term
        power = power * span
    return total


def rotated_faces(turn_w, orientation, integrals, put):
    result = matmul_each(turn_w[...], [tall_basis(value) for value in integrals])
    for q in range(QUANTITIES):
        for g in range(FACES):
            turn = orientation[g : g + 1, :]
            parts = []
            for o in range(3):
                first = (o * FACES + g) * FACE_PAD
                parts.append(result[q][first : first + FACE_PAD, :])
            put(g, q, jnp.where(turn == 0, parts[0], jnp.where(turn == 1, parts[1], parts[2])))


def rows_of(q):
    return slice(q * FACE_PAD, (q + 1) * FACE_PAD)


def take_lanes(source, index):
    if source.shape[0] == 1:
        return take_lanes(jnp.broadcast_to(source, (8, LANES)), index)[0:1, :]
    return jnp.take_along_axis(source, jnp.broadcast_to(index, source.shape), axis=1)


def turn_lanes(x, shift):
    return pltpu.roll(x, shift % LANES, 1) if shift % LANES else x


def choose(pieces, lane, width):
    total = pieces[0]
    for j in range(1, len(pieces)):
        total = jnp.where(lane // width == j, pieces[j], total)
    return total


def pack_sends(faces, index, sends):
    tiles = []
    for row in (0, 2):
        lane = index[row : row + 1, :]
        face = index[row + 1 : row + 2, :]
        tile = take_lanes(faces[0], lane)
        for g in range(1, FACES):
            tile = jnp.where(face == g, take_lanes(faces[g], lane), tile)
        tiles.append(tile)
    lane = lax.broadcasted_iota(jnp.int32, (FACE_PAD, LANES), 1)
    nothing = jnp.zeros((FACE_PAD, LANES), F32)

    def piece(tile, q):
        return tiles[tile][rows_of(q), :] if q < QUANTITIES else nothing

    for k in range(5):
        low, high = piece(0, 2 * k), piece(0, 2 * k + 1)
        sends[0][rows_of(k), :] = choose([low, turn_lanes(high, 64)], lane, 64)
        sends[1][rows_of(k), :] = choose([turn_lanes(low, 64), high], lane, 64)
    for k in range(5):
        for side in range(2):
            value = nothing
            if k < PACKS:
                parts = [turn_lanes(piece(1, 4 * k + j), 32 * j - 64 * side) for j in range(4)]
                value = choose(parts, lane, 32)
            sends[2 + side][rows_of(k), :] = value


def unpack_receives(receives, near, far):
    lane = lax.broadcasted_iota(jnp.int32, (FACE_PAD, LANES), 1)
    for q in range(QUANTITIES):
        ahead, behind = receives[0][rows_of(q // 2), :], receives[1][rows_of(q // 2), :]
        shift = 64 * (q % 2)
        near[rows_of(q), :] = choose([turn_lanes(ahead, shift), turn_lanes(behind, 64 + shift)], lane, 64)
        ahead, behind = receives[2][rows_of(q // 4), :], receives[3][rows_of(q // 4), :]
        shift = -32 * (q % 4)
        far[rows_of(q), :] = choose([turn_lanes(ahead, shift), turn_lanes(behind, 64 + shift)], lane, 64)


def add_remote(index, near, far, collected, put):
    for f in range(FACES):
        place = index[f : f + 1, :]
        lane = jnp.bitwise_and(place, LANES - 1)
        from_near = take_lanes(near[...], lane)
        from_far = take_lanes(far[...], lane)
        remote = jnp.where(place >= LANES, from_far, jnp.where(place >= 0, from_near, 0.0))
        put(f, collected[f] + remote)


def transposed(rows, flip):
    flip[...] = jnp.zeros((LANES, LANES), F32)
    for f in range(FACES):
        flip[f : f + 1, :] = rows[f]
    return flip[...].T


def ranks(keys, flip):
    columns = transposed(keys, flip)
    result = []
    for f in range(FACES):
        total = None
        for other in range(FACES):
            less = jnp.where(columns[:, other : other + 1] < keys[f], 1.0, 0.0)
            total = less if total is None else total + less
        result.append(jnp.sum(total, axis=0, keepdims=True))
    return result


def group_places(groups, keys, flip):
    bases = (0.0, 64.0, 128.0, 192.0)
    order = ranks([groups[f] * 512.0 + keys[f] for f in range(FACES)], flip)
    sizes = []
    for partner in range(FACES):
        total = None
        for f in range(FACES):
            here = jnp.where(groups[f] == partner, 1.0, 0.0)
            total = here if total is None else total + here
        sizes.append(jnp.sum(total, axis=1, keepdims=True))
    places = []
    for f in range(FACES):
        place = jnp.full((1, LANES), -1.0, F32)
        start = jnp.zeros((1, 1), F32)
        for partner in range(FACES):
            place = jnp.where(groups[f] == partner, order[f] - start + bases[partner], place)
            start = start + sizes[partner]
        places.append(place)
    return places


def send_places(groups, scratch):
    row = lax.broadcasted_iota(jnp.int32, (LANES, LANES), 0)
    lane = lax.broadcasted_iota(jnp.int32, (LANES, LANES), 1)
    earlier = jnp.where(row < lane, 1.0, 0.0).astype(BF16)
    for f in range(FACES):
        for partner in range(4):
            scratch[4 * f + partner : 4 * f + partner + 1, :] = jnp.where(groups[f] == partner, 1.0, 0.0)
    members = scratch[0:16, :]
    before = matmul(members, earlier)
    totals = jnp.sum(members, axis=1, keepdims=True)
    starts = [64.0 * partner for partner in range(4)]
    places = []
    for f in range(FACES):
        place = jnp.full((1, LANES), -1.0, F32)
        for partner in range(4):
            i = 4 * f + partner
            place = jnp.where(groups[f] == partner, before[i : i + 1, :] + starts[partner], place)
            starts[partner] = starts[partner] + totals[i : i + 1, :]
        places.append(place)
    return places


def partner_groups(devices, neighbour, face_kind):
    here = lax.axis_index("dom")
    sign = 1 - 2 * jnp.bitwise_and(here, 1)
    targets = [jnp.where(sign * by < 0, sign * by + devices, sign * by) for by in OFFSETS]
    sources = targets[:2] + [devices - far for far in targets[2:]]
    send_groups, recv_groups, local = [], [], []
    for f in range(FACES):
        interior = face_kind[f : f + 1, :] == 0
        distance = lax.shift_right_logical(neighbour[f : f + 1, :], 7) - here
        distance = jnp.where(distance < 0, distance + devices, distance)
        send = jnp.full((1, LANES), 4, jnp.int32)
        recv = jnp.full((1, LANES), 4, jnp.int32)
        for partner in range(4):
            send = jnp.where(interior & (distance == targets[partner]), partner, send)
            recv = jnp.where(interior & (distance == sources[partner]), partner, recv)
        send_groups.append(send.astype(F32))
        recv_groups.append(recv.astype(F32))
        local.append(interior & (distance == 0))
    return send_groups, recv_groups, local


def make_send_index(devices, neighbour, face_kind, index, flip, spare):
    groups, _, _ = partner_groups(devices, neighbour, face_kind)
    places = send_places(groups, flip)
    for tile, (element, face) in enumerate(columns_of(places, spare)):
        index[2 * tile : 2 * tile + 1, :] = element
        index[2 * tile + 1 : 2 * tile + 2, :] = face


def columns_of(places, flip):
    columns = transposed(places, flip)
    row = lax.broadcasted_iota(jnp.int32, (LANES, LANES), 0).astype(F32)
    lane = lax.broadcasted_iota(jnp.int32, (LANES, LANES), 1).astype(F32)
    result = []
    for tile in range(2):
        total = None
        for f in range(FACES):
            hit = jnp.where(columns[:, f : f + 1] == lane + tile * 128.0, row + f * 128.0, 0.0)
            total = hit if total is None else total + hit
        code = jnp.sum(total, axis=0, keepdims=True).astype(jnp.int32)
        result.append((jnp.bitwise_and(code, LANES - 1), lax.shift_right_logical(code, 7)))
    return result


def make_recv_index(devices, neighbour, neighbour_face, face_kind, index, flip):
    _, groups, local = partner_groups(devices, neighbour, face_kind)
    index[...] = jnp.zeros((24, LANES), jnp.int32)
    keys = []
    for f in range(FACES):
        far_face = neighbour_face[f : f + 1, :]
        far_element = jnp.bitwise_and(neighbour[f : f + 1, :], LANES - 1)
        keys.append((far_face * LANES + far_element).astype(F32))
        index[8 + f : 9 + f, :] = far_element
        index[16 + f : 17 + f, :] = jnp.where(local[f], far_face, -1)
    places = group_places(groups, keys, flip)
    for f in range(FACES):
        index[f : f + 1, :] = places[f].astype(jnp.int32)


def make_deriv(deriv, frame, deriv_w):
    deriv_w[...] = frame[...]
    for d in range(3):
        deriv_w[d * BASIS_PAD : d * BASIS_PAD + BASIS, :BASIS] = -deriv[d]
    deriv_w[...] = wide_basis(deriv_w[...])


def make_faces(proj, orient, frame, proj_w, turn_w, flip):
    proj_w[...] = frame[0:64, :]
    for g in range(FACES):
        proj_w[g * FACE_PAD : g * FACE_PAD + FACE_BASIS, :BASIS] = proj[:, g, :]
    right = side_by_side([proj_w[rows_of(g), :] for g in range(FACES)])
    flip[...] = frame[...]
    for o in range(3):
        flip[o * FACE_PAD : o * FACE_PAD + FACE_BASIS, :FACE_BASIS] = orient[o]
    turned = jnp.dot(
        flip[0:48, :FACE_PAD], right, precision=lax.Precision.HIGHEST, preferred_element_type=F32
    )
    for o in range(3):
        for g in range(FACES):
            turn_w[rows_of(o * FACES + g), :] = wide_basis(turned[rows_of(o), lanes_of(g)])
    proj_w[...] = wide_basis(proj_w[...])


def make_update(update, update_w, flips):
    update_w[...] = jnp.zeros((LANES, LANES), F32)
    for d in range(3):
        flip = flips.at[d]
        flip[...] = jnp.zeros((LANES, LANES), F32)
        flip[:BASIS, :BASIS] = update[d]
        update_w[d * BASIS_PAD : (d + 1) * BASIS_PAD, :] = flip[...].T[:BASIS_PAD, :]
    update_w[...] = wide_basis(update_w[...])


def make_lift(lift_mat, deriv_w, lift_w, flips):
    total = None
    for f in range(FACES):
        flip = flips.at[f]
        flip[...] = jnp.zeros((LANES, LANES), F32)
        flip[:FACE_BASIS, :BASIS] = lift_mat[:, f, :]
        value = turn_lanes(flip[...].T[0:48, :], 16 * f)
        total = value if total is None else total + value
    lift_w[0:48, :] = wide_faces(total)
    lift_w[48:176, :] = wide_faces(matmul(deriv_w[...], tall_basis(total[0:BASIS_PAD, :])))


def pack(pieces, element, lane):
    return choose([take_lanes(piece, element) for piece in pieces], lane, PACK)


def pack_quantities(pieces, element):
    lane = lax.broadcasted_iota(jnp.int32, pieces[0].shape, 1)
    nothing = jnp.zeros(pieces[0].shape, F32)
    result = []
    for k in range(PACKS):
        group = [take_lanes(pieces[q], element) if q < QUANTITIES else nothing for q in range(4 * k, 4 * k + 4)]
        result.append(choose(group, lane, PACK))
    return result


def unpack_quantity(packed, q, rank):
    return take_lanes(packed(q // 4), rank + PACK * (q % 4))


def make_packs(r):
    row = lax.broadcasted_iota(jnp.int32, (LANES, LANES), 0).astype(F32)
    lane = lax.broadcasted_iota(jnp.int32, (LANES, LANES), 1)
    cluster = r.cluster[...].astype(F32)
    columns = transposed([cluster] * FACES, r.flips.at[8])
    before = jnp.where((columns[:, 0:1] == cluster) & (row < lane.astype(F32)), 1.0, 0.0)
    rank = jnp.sum(before, axis=0, keepdims=True)
    columns = transposed([cluster * 64.0 + rank] * FACES, r.flips.at[9])
    r.packs[...] = jnp.zeros((8, LANES), jnp.int32)
    for block in range(2):
        wanted = jnp.bitwise_and(lane, PACK - 1).astype(F32) + 64.0 * block
        hit = jnp.where(columns[:, 0:1] == wanted, row, 0.0)
        r.packs[block : block + 1, :] = jnp.sum(hit, axis=0, keepdims=True).astype(jnp.int32)
    rank = rank.astype(jnp.int32)
    r.packs[2:3, :] = jnp.bitwise_and(rank, PACK - 1)
    lane = lax.broadcasted_iota(jnp.int32, (1, LANES), 1)
    kinds = r.cluster[...]
    for tile in range(2):
        element = r.send_index[2 * tile : 2 * tile + 1, :]
        face = r.send_index[2 * tile + 1 : 2 * tile + 2, :]
        kind = take_lanes(kinds, element)
        order = take_lanes(jnp.bitwise_and(rank, PACK - 1), element)
        rows = [order] + [jnp.where(kind == block, face, -1) for block in range(2)]
        for side in range(2):
            width = 32 if tile else 64
            for i in range(3):
                parts = [turn_lanes(rows[i], width * j - 64 * side) for j in range(LANES // width)]
                value = choose(parts, lane, width)
                if i == 0:
                    value = value + PACK * (lane // width)
                first = 3 * (2 * tile + side) + i
                r.send_packs[first : first + 1, :] = value


def make_targets(r):
    kinds = r.cluster[...]
    lane = lax.broadcasted_iota(jnp.int32, (1, LANES), 1)
    for f in range(FACES):
        r.source_cluster[f : f + 1, :] = take_lanes(kinds, r.index[8 + f : 9 + f, :])
    got = [r.index[f : f + 1, :].astype(F32) for f in range(FACES)]
    for tile, (element, _) in enumerate(columns_of(got, r.flip)):
        kind = take_lanes(kinds, element)
        for side in range(2):
            width = 32 if tile else 64
            parts = [turn_lanes(kind, width * j - 64 * side) for j in range(LANES // width)]
            first = 2 * tile + side
            r.column_cluster[first : first + 1, :] = choose(parts, lane, width)


def pack_flux(flux, element, packed):
    lane = lax.broadcasted_iota(jnp.int32, (FACES, LANES), 1)
    face = lax.broadcasted_iota(jnp.int32, (FACES, LANES), 0)
    for q in range(QUANTITIES):
        for p in range(QUANTITIES):
            value = jnp.where(face == lane // PACK, take_lanes(flux[q, p], element), 0.0)
            packed[q, p : p + 1, :] = jnp.sum(value, axis=0, keepdims=True)


def pack_block(r, block, where, star, flux):
    element = r.packs[block : block + 1, :]
    lane = lax.broadcasted_iota(jnp.int32, (1, LANES), 1)
    where[...] = jnp.zeros((8, LANES), jnp.int32)
    where[0:1, :] = pack([r.index[f : f + 1, :] for f in range(FACES)], element, lane)
    where[1:5, :] = take_lanes(r.orientation[...], element)
    where[5:6, :] = pack([r.index[8 + f : 9 + f, :] for f in range(FACES)], element, lane)
    where[6:7, :] = pack([r.index[16 + f : 17 + f, :] for f in range(FACES)], element, lane)
    for q in range(QUANTITIES):
        for k, value in enumerate(pack_quantities([r.star[q, p] for p in range(QUANTITIES)], element)):
            star[q, k] = value
    pack_flux(r.flux_neigh, element, flux)


def spread_faces(total, lift_in):
    lane = lax.broadcasted_iota(jnp.int32, (FACE_PAD, LANES), 1)
    nothing = jnp.zeros((FACE_PAD, LANES), F32)
    for k in range(PACKS):
        group = [total[q] if q < QUANTITIES else nothing for q in range(GROUPS * k, GROUPS * (k + 1))]
        turned = [turn_lanes(value, PACK * shift) for shift, value in enumerate(rotated_by_copy(group, lane))]
        placed = rotated_by_copy(turned, lane)
        for f in range(FACES):
            lift_in[f * FACE_PAD : (f + 1) * FACE_PAD, lanes_of(k)] = placed[(GROUPS - f) % GROUPS]
    return [tall_faces(lift_in[:, lanes_of(k)]) for k in range(PACKS)]


def received_piece(refs, place, p):
    near, far = jnp.bitwise_and(place, 63), jnp.bitwise_and(place, PACK - 1)
    got = [take_lanes(ref[rows_of(p // 2), :], near + 64 * (p % 2)) for ref in refs[:2]]
    got += [take_lanes(ref[rows_of(p // 4), :], far + PACK * (p % 4)) for ref in refs[2:]]
    got = jnp.where(place < 128, jnp.where(place < 64, got[0], got[1]), jnp.where(place < 192, got[2], got[3]))
    return jnp.where(place >= 0, got, 0.0)


def flux_sum(flux, pieces):
    total = [None] * QUANTITIES
    for p in range(QUANTITIES):
        for q in range(QUANTITIES):
            term = flux(q, p) * pieces[p]
            total[q] = term if total[q] is None else total[q] + term
    return total


def packed_fields(r, block, base, ahead, gathered, flux, where, lift_in, work):
    refs = [getattr(r, ("sum_" if block else "got_") + name) for name in "axyz"]
    place = where[0:1, :]
    pieces = [gathered[rows_of(p), :] + received_piece(refs, place, p) for p in range(QUANTITIES)]
    total = flux_sum(lambda q, p: flux[q, p : p + 1, :], pieces)
    lifted = matmul_each(r.lift_w[:, :192], spread_faces(total, lift_in), 1)
    for k in range(PACKS):
        work[:, lanes_of(k)] = ahead[:, lanes_of(k)] - lifted[k][48:176, :]
    return [base[k] - lifted[k][:BASIS_PAD, :] for k in range(PACKS)]


def packed_derivatives(terms, deriv_w, work):
    for k in range(PACKS):
        work[:, lanes_of(k)] = matmul(deriv_w[...], tall_basis(terms[k]))


def rotated_by_copy(values, lane):
    odd, high = jnp.bitwise_and(lane, PACK) != 0, lane >= 2 * PACK
    step = [jnp.where(odd, values[(i + 1) % GROUPS], values[i]) for i in range(GROUPS)]
    return [jnp.where(high, step[(i + 2) % GROUPS], step[i]) for i in range(GROUPS)]


def gather_copies(values):
    lane = lax.broadcasted_iota(jnp.int32, (BASIS_PAD, LANES), 1)
    if len(values) == 1:
        value = values[0]
        rolled = [pltpu.roll(value, PACK * shift, 1) for shift in (1, 2, 3)]
        return jnp.where(lane < PACK, (value + rolled[0]) + (rolled[1] + rolled[2]), 0.0)
    mixed = rotated_by_copy(values, lane)
    parts = [turn_lanes(mixed[shift], PACK * shift) for shift in range(GROUPS)]
    return (parts[0] + parts[1]) + (parts[2] + parts[3])


def packed_star(star, work, k):
    quantities = range(GROUPS * k, min(GROUPS * (k + 1), QUANTITIES))
    return gather_copies(star_tile(star, work, quantities, PACKS))


def packed_faces(integrals, turn_w, where, put):
    result = matmul_each(turn_w[...], [tall_basis(value) for value in integrals], 1)
    for k in range(PACKS):
        for g in range(FACES):
            turn = where[1 + g : 2 + g, :]
            parts = [result[k][rows_of(o * FACES + g), :] for o in range(3)]
            put(g, k, jnp.where(turn == 0, parts[0], jnp.where(turn == 1, parts[1], parts[2])))


def add_terms(total, terms, weight):
    values = [term * weight for term in terms]
    return values if total is None else [a + b for a, b in zip(total, values)]


def add_received(r):
    for name in "axyz":
        getattr(r, "sum_" + name)[...] = getattr(r, "got_" + name)[...] + getattr(r, "old_" + name)[...]


def slot_kernel(slot, r):
    if slot == 2:
        add_received(r)
    numbers = (0, 1) if slot == 2 else (0,)
    names = ("base", "ahead", "gathered", "flux", "where", "lift_in", "star", "fields", "step", "faces", "work", "spare")
    blocks = [types.SimpleNamespace(**{name: getattr(r, name + str(b)) for name in names}) for b in numbers]
    terms = []
    for b, block in enumerate(blocks):
        terms.append(
            packed_fields(
                r, b, block.base, block.ahead, block.gathered, block.flux, block.where, block.lift_in, block.work
            )
        )
        for k in range(PACKS):
            block.fields[k] = terms[-1][k]
    first = [None] * len(blocks)
    second = None
    for k in range(ORDER):
        for i in range(PACKS if k else 0):
            for b, block in enumerate(blocks):
                work, other = (block.work, block.spare) if k % 2 else (block.spare, block.work)
                terms[b][i] = packed_star(block.star, work, i)
                if k < ORDER - 1:
                    other[:, lanes_of(i)] = matmul(r.deriv_w[...], tall_basis(terms[b][i]))
        for b in range(len(blocks)):
            first[b] = add_terms(first[b], terms[b], 1.0 / math.factorial(k + 1))
        if slot == 2:
            second = add_terms(second, terms[1], (2.0 ** (k + 1) - 1.0) / math.factorial(k + 1))
    for b, block in enumerate(blocks):

        def put(g, k, value, faces=block.faces):
            faces[g, rows_of(k), :] = value

        packed_faces(first[b], r.turn_w, block.where, put)
        for k in range(PACKS):
            block.step[k] = first[b][k]
    if slot == 2:
        for k in range(PACKS):
            r.second1[k] = second[k]
    for partner in SEND_ORDER:
        later, sent = getattr(r, "later_" + NAMES[partner]), getattr(r, NAMES[partner])
        near = partner < 2
        lane = r.send_packs[3 * partner : 3 * partner + 1, :]
        for k in range(5 if near else PACKS):
            value = later[rows_of(k), :]
            source = k // 2 if near else k
            place = lane + 64 * (k % 2) if near else lane
            for b, block in enumerate(blocks):
                face = r.send_packs[3 * partner + 1 + b : 3 * partner + 2 + b, :]
                for g in range(FACES):
                    value = jnp.where(face == g, take_lanes(block.faces[g, rows_of(source), :], place), value)
            sent[rows_of(k), :] = value
        if not near:
            sent[48:80, :] = jnp.zeros((32, LANES), F32)


def frame_kernel(r):
    r.frame[...] = jnp.zeros((LANES, LANES), F32)


def first_kernel(devices, r):
    make_deriv(r.deriv, r.frame, r.deriv_w)
    for q in range(QUANTITIES):
        r.taylor[0, q] = jnp.zeros((BASIS_PAD, LANES), F32)
        r.taylor[0, q, :BASIS, :] = r.dofs[q]
    r.orientation_out[...] = r.orientation[...]
    r.cluster_out[...] = r.cluster[...].reshape(1, LANES)
    r.far_out[...] = r.neighbour_face[...]
    between = {
        1: lambda: make_send_index(devices, r.neighbour, r.face_kind, r.send_index, r.flip, r.flap),
        2: lambda: make_faces(r.proj, r.orient, r.frame, r.proj_w, r.turn_w, r.flop),
    }
    predict(r.taylor, r.star, r.deriv_w, (r.spare, r.work), between)
    span = lax.shift_left(jnp.ones_like(r.cluster_out[...]), r.cluster_out[...]).astype(F32)
    for q in range(QUANTITIES):
        r.step[q] = step_integral(r.taylor, q, span)

    def put(g, q, value):
        r.faces[g, rows_of(q), :] = value

    rotated_faces(r.turn_w, r.orientation, [integral(r.taylor, q, 0) for q in range(QUANTITIES)], put)
    pack_sends(r.faces, r.send_index, [getattr(r, name) for name in NAMES])


def last_kernel(r):
    unpack_receives([getattr(r, name) for name in RECEIVED], r.near, r.far)

    def keep(f, value):
        r.collected[f] = value

    add_remote(r.index, r.near, r.far, r.gathered, keep)
    apply_flux(r.flux_neigh, lambda f, p: r.collected[f, rows_of(p), :], r.lift_in)
    lifted = lift(r.lift_w, r.lift_in)
    for q in range(QUANTITIES):
        r.out[q] = (r.base[q] - lifted[q][:BASIS_PAD, :])[:BASIS, :]


def later_faces(r, j, later):
    def store(g, q, value):
        later[g, rows_of(q), :] = value

    rotated_faces(r.turn_w, r.orientation, [integral(r.taylor, q, j) for q in range(QUANTITIES)], store)


def beside_kernel(slot, devices, r):
    if slot == 0:
        make_update(r.update, r.update_w, r.flips.at[0:3])
        make_lift(r.lift_mat, r.deriv_w, r.lift_w, r.flips.at[3:7])
        make_recv_index(devices, r.neighbour, r.neighbour_face, r.face_kind, r.index, r.flips.at[7])
        make_packs(r)
        pack_block(r, 0, r.where0, r.star0, r.flux0)
        mirror = jnp.where(r.face_kind[...] == 1, 1.0, 0.0)
        for p in range(QUANTITIES):
            sign = -mirror if p < 6 else mirror
            for q in range(QUANTITIES):
                r.flux_own[q, p] = r.flux_local[q, p] + sign * r.flux_neigh[q, p]
    cluster = r.cluster[...]
    started = cluster <= (0 if slot % 2 else 1)
    rank = r.packs[2:3, :]

    def unpacked(name, q, rows=None):
        def packed(ref):
            return (lambda k: ref[k]) if rows is None else (lambda k: ref[rows, rows_of(k), :])

        value = unpack_quantity(packed(getattr(r, name + "0")), q, rank)
        if slot == 2:
            value = jnp.where(cluster == 1, unpack_quantity(packed(getattr(r, name + "1")), q, rank), value)
        return value

    sums = r.sums if slot else r.faces
    if slot == 1:
        make_targets(r)
    for g in range(FACES if slot else 0):
        reset = r.source_cluster[g : g + 1, :] <= (0 if slot % 2 else 1)
        for q in range(QUANTITIES):
            value = jnp.where(started, unpacked("faces", q, g), r.later[g, rows_of(q), :])
            sums[g, rows_of(q), :] = value + jnp.where(reset, 0.0, r.old_sums[g, rows_of(q), :])
    if slot:
        for i, name in enumerate("axyz"):
            reset = r.column_cluster[i : i + 1, :] <= (0 if slot % 2 else 1)
            total = getattr(r, "sum_" + name)[...] if slot == 2 else getattr(r, "got_" + name)[...]
            if slot == 3:
                total = total + getattr(r, "older_" + name)[...]
            getattr(r, "old_" + name)[...] = jnp.where(reset, 0.0, total)
    if slot == 3:
        for f in range(FACES):
            lane = r.index[8 + f : 9 + f, :]
            face = r.index[16 + f : 17 + f, :]
            total = None
            for g in range(FACES):
                value = jnp.where(face == g, take_lanes(sums[g], lane), 0.0)
                total = value if total is None else total + value
            r.gathered[f] = total
        unpack_receives([r.old_a, r.old_x, r.old_y, r.old_z], r.near, r.far)

        def keep(f, value):
            r.gathered[f] = value

        add_remote(r.index, r.near, r.far, r.gathered, keep)
    if slot == 0:
        fields = [r.taylor[0, q] for q in range(QUANTITIES)]
        steps = [r.step[q] for q in range(QUANTITIES)]
    else:
        fields = [unpacked("fields", q) for q in range(QUANTITIES)]
        steps = [unpacked("step", q) for q in range(QUANTITIES)]
        if slot == 2:
            for q in range(QUANTITIES):
                steps[q] = steps[q] + jnp.where(cluster == 1, unpack_quantity(lambda k: r.second1[k], q, rank), 0.0)
    right = [tall_basis(value) for value in steps]
    own = matmul_each(r.proj_w[...], right)
    apply_flux(r.flux_own, lambda f, p: own[p][rows_of(f), :], r.lift_in)
    lifted = lift(r.lift_w, r.lift_in)
    for q, value in enumerate(matmul_each(r.update_w[...], right)):
        r.work[:, lanes_of(q)] = value

    def put(q, value):
        value = fields[q] + value - lifted[q][:BASIS_PAD, :]
        r.base[q] = value if slot == 0 else jnp.where(started, value, r.old_base[q])

    apply_star(r.star, r.work, put)
    if slot == 1:
        pack_block(r, 1, r.where1, r.star1, r.flux1)
    if slot == 0:
        later_faces(r, 1, r.later1)
    if slot == 1:
        later_faces(r, 2, r.later2)
        later_faces(r, 3, r.later3)
    if slot == 2:

        def merge(g, q, value):
            r.next_later[g, rows_of(q), :] = jnp.where(cluster == 1, value, r.after[g, rows_of(q), :])

        rotated_faces(
            r.turn_w,
            r.orientation,
            [unpack_quantity(lambda k: r.second1[k], q, rank) for q in range(QUANTITIES)],
            merge,
        )
    if slot == 3:
        return
    later = r.later1 if slot == 0 else r.later2 if slot == 1 else r.next_later
    pack_sends(later, r.send_index, [getattr(r, "later_" + name) for name in NAMES])
    targets = [(r.base0, r.ahead0, r.gathered0, r.where0)]
    if slot == 1:
        targets.append((r.base1, r.ahead1, r.gathered1, r.where1))
    for block, (base, ahead, gathered, where) in enumerate(targets):
        packed = pack_quantities([r.base[q] for q in range(QUANTITIES)], r.packs[block : block + 1, :])
        for k in range(PACKS):
            base[k] = packed[k]
        packed_derivatives(packed, r.deriv_w, ahead)
        lane, face = where[5:6, :], where[6:7, :]
        total = None
        for g in range(FACES):
            value = jnp.where(face == g, take_lanes(sums[g], lane), 0.0)
            total = value if total is None else total + value
        gathered[...] = total


def shape_of(array):
    return jax.ShapeDtypeStruct(array.shape, array.dtype)


def shape(*dims):
    return jax.ShapeDtypeStruct(dims, F32)


def ints(rows):
    return jax.ShapeDtypeStruct((rows, LANES), jnp.int32)


RECEIVED = ("got_a", "got_x", "got_y", "got_z")
TAYLOR = shape(ORDER, QUANTITIES, BASIS_PAD, LANES)
STATE = shape(QUANTITIES, BASIS_PAD, LANES)
PACKED = shape(PACKS, BASIS_PAD, LANES)
AHEAD = shape(LANES, PACKS * LANES)
PACKED_STAR = shape(QUANTITIES, PACKS, 3, LANES)
PACKED_FLUX = shape(QUANTITIES, QUANTITIES, LANES)
PACKED_LIFT = shape(FACES * FACE_PAD, PACKS * LANES)
TURNED = shape(FACES, FACE_ROWS, LANES)
TILE = shape(FACE_ROWS, LANES)
SQUARE = shape(LANES, LANES)
WORK = shape(LANES, QUANTITIES * LANES)
LIFT_IN = shape(FACES * FACE_PAD, QUANTITIES * LANES)
SENDS = {NAMES[i]: shape(SEND_ROWS, LANES) for i in SEND_ORDER}
OLD = {"old_" + name: shape(SEND_ROWS, LANES) for name in "axyz"}
SUMS = {"sum_" + name: shape(SEND_ROWS, LANES) for name in "axyz"}
LATER_SENDS = {"later_" + name: value for name, value in SENDS.items()}
EARLY_FLOPS = 5_000_000_000


def call(kernel, name, ins, outs, scratch, flops):
    names = [*ins, *outs, *scratch]
    size = sum(math.prod(a.shape) * 4 for a in [*ins.values(), *outs.values()])

    def run(*refs):
        kernel(types.SimpleNamespace(**dict(zip(names, refs))))

    result = pl.pallas_call(
        run,
        out_shape=list(outs.values()),
        in_specs=[VMEM] * len(ins),
        out_specs=[VMEM] * len(outs),
        scratch_shapes=[pltpu.VMEM(a.shape, a.dtype) for a in scratch.values()],
        compiler_params=pltpu.CompilerParams(vmem_limit_bytes=32 * 1024 * 1024),
        cost_estimate=pl.CostEstimate(flops=flops, bytes_accessed=size, transcendentals=0),
        name=name,
    )(*ins.values())
    return dict(zip(outs, result))


def some(values, *names):
    return {name: values[name] for name in names}


def body(
    dofs, star, flux_local, flux_neigh, neighbour, neighbour_face, orientation, face_kind, cluster,
    deriv_stiff, update_stiff, face_proj, face_lift, orient_map,
):
    devices = lax.axis_size("dom")
    star, flux_local, flux_neigh = [jnp.transpose(a, (1, 2, 0, 3)) for a in (star, flux_local, flux_neigh)]
    face_proj, face_lift = jnp.transpose(face_proj, (1, 0, 2)), jnp.transpose(face_lift, (2, 0, 1))
    v = dict(
        star=star, flux_local=flux_local, flux_neigh=flux_neigh, neighbour=neighbour,
        face_kind=face_kind, update=update_stiff, lift_mat=face_lift,
    )
    frame = call(frame_kernel, "frame", {}, dict(frame=SQUARE), {}, EARLY_FLOPS)["frame"]
    sends = call(
        functools.partial(first_kernel, devices),
        "start",
        dict(frame=frame, neighbour=neighbour, neighbour_face=neighbour_face, face_kind=face_kind,
             orientation=orientation, cluster=cluster, deriv=deriv_stiff, proj=face_proj, orient=orient_map,
             dofs=dofs, star=star),
        dict(deriv_w=SQUARE, far_out=ints(FACES), proj_w=shape(64, LANES), turn_w=shape(192, LANES),
             send_index=ints(8), orientation_out=ints(FACES), cluster_out=ints(1),
             taylor=TAYLOR, step=STATE, faces=TURNED, **SENDS),
        dict(work=WORK, spare=WORK, flip=SQUARE, flap=SQUARE, flop=SQUARE),
        100_000_000,
    )
    v.update(some(sends, "deriv_w", "proj_w", "turn_w", "send_index"), orientation=sends["orientation_out"],
             cluster=sends["cluster_out"], neighbour_face=sends["far_out"])
    receives = exchange(sends)
    kept = call(
        functools.partial(beside_kernel, 0, devices),
        "beside0",
        {**some(sends, "taylor", "step", "faces"),
         **some(v, "star", "orientation", "cluster", "flux_local", "flux_neigh", "face_kind", "neighbour",
                "neighbour_face", "update", "lift_mat", "deriv_w", "proj_w", "turn_w", "send_index")},
        dict(base=STATE, flux_own=shape_of(flux_local), later1=TURNED, update_w=SQUARE, lift_w=shape(176, 256), index=ints(24), packs=ints(8),
             send_packs=ints(12), where0=ints(8), star0=PACKED_STAR, flux0=PACKED_FLUX,
             base0=PACKED, ahead0=AHEAD, gathered0=TILE, **LATER_SENDS),
        dict(work=WORK, lift_in=LIFT_IN, flips=shape(10, LANES, LANES)),
        50_000_000,
    )
    v.update(kept)
    v.update(taylor=sends["taylor"], sums=sends["faces"])
    for slot in range(1, SLOTS):
        numbers = (0, 1) if slot == 2 else (0,)
        per_block = [name + str(b) for b in numbers for name in ("base", "ahead", "gathered", "flux", "star", "where")]
        outs, scratch = {}, {}
        for b in numbers:
            outs.update({"fields%d" % b: PACKED, "step%d" % b: PACKED, "faces%d" % b: shape(FACES, 48, LANES)})
            scratch.update(
                {"work%d" % b: AHEAD, "spare%d" % b: AHEAD, "lift_in%d" % b: PACKED_LIFT}
            )
        if slot == 2:
            outs["second1"] = PACKED
        sends = call(
            functools.partial(slot_kernel, slot),
            "slot%d" % slot,
            {**receives, **(some(v, *OLD) if slot == 2 else {}),
             **some(v, *per_block, *LATER_SENDS, "deriv_w", "turn_w", "lift_w", "send_packs")},
            {**outs, **(SUMS if slot == 2 else {}), **SENDS},
            scratch,
            100_000_000,
        )
        previous, receives = receives, exchange(sends)
        ins = some(sends, *outs, *(SUMS if slot == 2 else ()))
        if slot != 2:
            ins.update(previous)
        if slot == 3:
            ins.update({"older_" + name: v["old_" + name] for name in "axyz"})
        ins.update(old_base=v["base"], old_sums=v["sums"], later=v["later%d" % slot])
        ins.update(
            some(v, "star", "cluster", "flux_own", "proj_w", "update_w", "lift_w", "packs")
        )
        results = dict(base=STATE, **(OLD if slot < 3 else {}))
        scratch = dict(work=WORK, lift_in=LIFT_IN)
        if slot < 3:
            ins.update(some(v, "send_index", "deriv_w", "where0"))
            results.update(sums=TURNED, base0=PACKED, ahead0=AHEAD, gathered0=TILE, **LATER_SENDS)
        else:
            ins.update(some(v, "index"))
            results.update(gathered=TURNED)
            scratch.update(sums=TURNED, near=TILE, far=TILE, **OLD)
        if slot > 1:
            ins.update(some(v, "source_cluster", "column_cluster"))
        if slot == 1:
            scratch.update(flip=SQUARE)
            results.update(source_cluster=ints(FACES), column_cluster=ints(4))
            ins.update(some(v, "flux_neigh", "orientation", "index", "turn_w", "taylor"))
            results.update(later2=TURNED, later3=TURNED, base1=PACKED, ahead1=AHEAD, gathered1=TILE, where1=ints(8), star1=PACKED_STAR,
                           flux1=PACKED_FLUX)
        if slot == 2:
            ins.update(after=v["later3"], **some(v, "orientation", "turn_w"))
            results.update(next_later=TURNED)
        v.update(
            call(
                functools.partial(beside_kernel, slot, devices), "beside%d" % slot, ins, results,
                scratch, 50_000_000,
            )
        )
        if slot == 2:
            v["later3"] = v["next_later"]
    return call(
        last_kernel,
        "finish",
        {**receives, **some(v, "base", "gathered", "flux_neigh", "lift_w", "index")},
        dict(out=shape(*dofs.shape)),
        dict(near=TILE, far=TILE, collected=TURNED, lift_in=LIFT_IN),
        10_000_000,
    )["out"]


def solution(mesh):
    in_specs = (
        P(None, None, "dom"),
        P(None, None, None, "dom"),
        P(None, None, None, "dom"),
        P(None, None, None, "dom"),
        P(None, "dom"),
        P(None, "dom"),
        P(None, "dom"),
        P(None, "dom"),
        P("dom"),
        P(),
        P(),
        P(),
        P(),
        P(),
    )
    out_specs = P(None, None, "dom")
    return jax.shard_map(body, mesh=mesh, in_specs=in_specs, out_specs=out_specs, check_vma=False)
```
